32 devices in a mesh: clip: 2 (over x), tm: 4 (over z), tensor: 4 (over y, core).
Axes of the slice: x: 2, y: 2, z: 4, core: 2. Of those that a mesh axis runs over, the one named last changes fastest.
Arguments:
- resid: bfloat16 [16, 4, 256, 6144], P('tm', 'clip', 'tensor'), parts along dimension 1, may hold values from -16 to 16
- spatial_q: bfloat16 [16, 4, 256, 3072], P('tm', 'clip', None, 'tensor'), parts along dimension 1, may hold values from -100 to 100
- spatial_k: bfloat16 [16, 4, 256, 3072], P('tm', 'clip', None, 'tensor'), parts along dimension 1, may hold values from -5 to 5
- spatial_v: bfloat16 [16, 4, 256, 3072], P('tm', 'clip', None, 'tensor'), parts along dimension 1, may hold values from -6 to 6
- out_weight: bfloat16 [3072, 6144], P('tensor'), may hold values from -0.109375 to 0.109375
- norm_gain: float32 [6144], replicated, may hold values from 0.1 to 1.9
- qkv_weight: bfloat16 [6144, 3, 3072], P('tm', None, 'tensor'), may hold values from -4 to 4
Outputs:
- resid_out: bfloat16 [16, 4, 256, 6144], P('tm', 'clip', 'tensor'), parts along dimension 1
- temporal_ctx: bfloat16 [16, 4, 256, 3072], P('tm', 'clip', None, 'tensor'), parts along dimension 1
The draws below stay inside these ranges and needn't reach their ends.
There are 2 independent parts, one for each index of `clip`. The reference program is written for one: setup_inputs(seed, part) draws one part's arguments, and reference() takes and returns one part's arrays. A program takes and returns all parts, laid end to end along the dimension named above; an argument that names none is the same for every part. Nothing has to cross between parts.
All inputs are finite; a program needn't handle non-finite values.
Results may differ from the reference program's by a relative error of at most 0.017.
Values may be sent and summed in bfloat16 or wider, within the bound.
No kernel may reach another device: no remote copies, remote signals or barrier semaphores. Data moves between devices by JAX's collectives and lax.ppermute only.
A program may use at most 320 MiB of HBM per device.

```python
import math
import jax
import jax.numpy as jnp
from jax import lax

D = 6144
HEADS = 24
HD = 128
PATCHES = 256
FRAMES = 16
CLIPS = 2
DH = 3072
N_TENSOR = 4


def draw_resid(key, part):
    dims_full = (FRAMES, CLIPS, PATCHES, D)
    first_key = jax.random.fold_in(jax.random.fold_in(key, 3), 0)
    noise_part = jax.random.normal(first_key, dims_full, jnp.float32)
    return jnp.clip(noise_part, -6.0, 6.0).astype(jnp.bfloat16)


def spatial_pair(key):
    key_list = jax.random.split(jax.random.fold_in(key, 7), 2)
    dims_full = (FRAMES, CLIPS, PATCHES, DH)
    key_base = jnp.clip(jax.random.normal(key_list[0], dims_full, jnp.float32), -4.0, 4.0)
    query_base = jnp.clip(jax.random.normal(key_list[1], dims_full, jnp.float32), -4.0, 4.0)
    return (query_base, key_base)


def draw_spatial_q(key, part):
    return spatial_pair(key)[0].astype(jnp.bfloat16)


def draw_spatial_k(key, part):
    return spatial_pair(key)[1].astype(jnp.bfloat16)


def draw_qkv_weight(key, part):
    key_list = jax.random.split(jax.random.fold_in(key, 5), 1)
    base = jnp.clip(jax.random.normal(key_list[0], (D, 3, DH), jnp.float32), -4.0, 4.0) / math.sqrt(D)
    return base.astype(jnp.bfloat16)


def level_of(rng, shape, shards, least, top_value):
    level, own = 1.0, jax.random.fold_in(rng, 6)
    for axis_at, blocks in shards:
        heights = jnp.exp(jax.random.uniform(jax.random.fold_in(own, axis_at), (blocks,), jnp.float32, least / len(shards), top_value / len(shards)))
        level = level * jnp.repeat(heights, shape[axis_at] // blocks).reshape([-1 if axis == axis_at else 1 for axis in range(len(shape))])
    return level


def noise(key, extent, deviation, most, cuts=(), kind=jnp.bfloat16):
    drawn = jax.random.normal(key, extent, jnp.float32) * deviation
    if len(cuts) > 0:
        drawn = level_of(key, extent, cuts, -0.22, 0.18) * drawn
    return jnp.clip(drawn, min=-most, max=most).astype(kind)


def setup_inputs(seed: int = 0, part: int = 0) -> dict:
    splits = jax.random.split(jax.random.key(seed), 8)
    part_splits = jax.random.split(jax.random.fold_in(splits[7], part), 8)
    resid = draw_resid(jax.random.fold_in(jax.random.fold_in(splits[7], part), 71), part)
    spatial_q = draw_spatial_q(jax.random.fold_in(jax.random.fold_in(splits[7], part), 71), part)
    spatial_k = draw_spatial_k(jax.random.fold_in(jax.random.fold_in(splits[7], part), 71), part)
    spatial_v = noise(part_splits[3], (FRAMES, CLIPS, PATCHES, DH), 1.0, 6.0, ((0, 4), (3, 4)))
    out_weight = noise(splits[4], (DH, D), DH ** -0.5, 0.109375, ((0, 4),))
    norm_gain = jnp.clip(1.0 + 0.18 * jax.random.normal(splits[5], (D,), jnp.float32), 0.1, 1.9)
    qkv_weight = draw_qkv_weight(jax.random.fold_in(splits[7], 71), part)
    return {"resid": resid, "spatial_q": spatial_q, "spatial_k": spatial_k, "spatial_v": spatial_v, "out_weight": out_weight, "norm_gain": norm_gain, "qkv_weight": qkv_weight}


def layer_norm(stream_in, norm_gain):
    average = lax.optimization_barrier(jnp.mean(stream_in, axis=-1, keepdims=True))
    centred = stream_in - average
    variance = lax.optimization_barrier(jnp.mean(centred * centred, axis=-1, keepdims=True))
    return (centred * lax.rsqrt(variance + 1e-06) * norm_gain.astype(jnp.float32)).astype(jnp.bfloat16)

def spatial_attend(queries, keys_in, values):
    head_shape = (FRAMES, CLIPS, PATCHES, HEADS, HD)
    query_heads = queries.astype(jnp.float32).reshape(head_shape)
    key_heads = keys_in.astype(jnp.float32).reshape(head_shape)
    value_heads = values.astype(jnp.float32).reshape(head_shape)
    scores = jnp.einsum('fcphd,fcqhd->fchpq', query_heads, key_heads) / math.sqrt(HD)
    weights = jax.nn.softmax(scores, axis=-1).astype(jnp.bfloat16)
    context = jnp.einsum('fchpq,fcqhd->fcphd', weights.astype(jnp.float32), value_heads)
    return context.astype(jnp.bfloat16).reshape(FRAMES, CLIPS, PATCHES, DH)

def temporal_attend(queries, keys_in, values):
    head_shape = (FRAMES, CLIPS, PATCHES, HEADS, HD)
    query_heads = queries.astype(jnp.float32).reshape(head_shape)
    key_heads = keys_in.astype(jnp.float32).reshape(head_shape)
    value_heads = values.astype(jnp.float32).reshape(head_shape)
    scores = jnp.einsum('fcphd,gcphd->cphfg', query_heads, key_heads) / math.sqrt(HD)
    weights = jax.nn.softmax(scores, axis=-1).astype(jnp.bfloat16)
    context = jnp.einsum('cphfg,gcphd->fcphd', weights.astype(jnp.float32), value_heads)
    return context.astype(jnp.bfloat16).reshape(FRAMES, CLIPS, PATCHES, DH)

def reference(resid, spatial_q, spatial_k, spatial_v, out_weight, norm_gain, qkv_weight):
    context = spatial_attend(spatial_q, spatial_k, spatial_v)
    flat_context = context.reshape(FRAMES * CLIPS * PATCHES, DH)
    group_width = DH // N_TENSOR
    running = jnp.zeros((FRAMES * CLIPS * PATCHES, D), jnp.float32)
    for member in range(N_TENSOR):
        context_block = flat_context[:, member * group_width:(member + 1) * group_width]
        weight_rows = out_weight[member * group_width:(member + 1) * group_width]
        partial_value = jnp.dot(context_block, weight_rows, preferred_element_type=jnp.float32).astype(jnp.bfloat16)
        partial_value = lax.optimization_barrier(partial_value)
        running = running + partial_value.astype(jnp.float32)
    stream = resid.astype(jnp.float32) + running.reshape(FRAMES, CLIPS, PATCHES, D)
    resid_out = stream.astype(jnp.bfloat16)
    normed = layer_norm(stream, norm_gain)
    projected = jnp.dot(normed.reshape(FRAMES * CLIPS * PATCHES, D), qkv_weight.reshape(D, 3 * DH), preferred_element_type=jnp.float32)
    projected = projected.astype(jnp.bfloat16).reshape(FRAMES, CLIPS, PATCHES, 3, DH)
    temporal_ctx = temporal_attend(projected[:, :, :, 0], projected[:, :, :, 1], projected[:, :, :, 2])
    return (resid_out, temporal_ctx)
```

```python
import functools
import math

import jax
import jax.numpy as jnp
from jax import lax
from jax.experimental import pallas as pl
from jax.experimental.pallas import tpu as pltpu
from jax.sharding import PartitionSpec as P

HD = 128
MIB = 1 << 20


def layer_norm(stream_in, norm_gain):
    average = jnp.mean(stream_in, axis=-1, keepdims=True)
    centred = stream_in - average
    variance = jnp.mean(centred * centred, axis=-1, keepdims=True)
    return (centred * lax.rsqrt(variance + 1e-06) * norm_gain).astype(jnp.bfloat16)


def spatial_attend(queries, keys_in, values):
    dims_in = queries.shape
    head_shape = dims_in[:3] + (dims_in[3] // HD, HD)
    query_heads = queries.reshape(head_shape)
    key_heads = keys_in.reshape(head_shape)
    value_heads = values.reshape(head_shape)
    scores = jnp.einsum(
        "fcphd,fcqhd->fchpq", query_heads, key_heads, preferred_element_type=jnp.float32
    ) / math.sqrt(HD)
    weights = jax.nn.softmax(scores, axis=-1).astype(jnp.bfloat16)
    context = jnp.einsum(
        "fchpq,fcqhd->fcphd", weights, value_heads, preferred_element_type=jnp.float32
    )
    return context.astype(jnp.bfloat16).reshape(dims_in)


def temporal_attend(queries, keys_in, values):
    query_dims = queries.shape
    heads_here = query_dims[3] // HD
    query_heads = queries.reshape(query_dims[:3] + (heads_here, HD))
    key_heads = keys_in.reshape(keys_in.shape[:3] + (heads_here, HD))
    value_heads = values.reshape(values.shape[:3] + (heads_here, HD))
    scores = jnp.einsum(
        "fcphd,gcphd->cphfg", query_heads, key_heads, preferred_element_type=jnp.float32
    ) / math.sqrt(HD)
    weights = jax.nn.softmax(scores, axis=-1).astype(jnp.bfloat16)
    context = jnp.einsum(
        "cphfg,gcphd->fcphd", weights, value_heads, preferred_element_type=jnp.float32
    )
    return context.astype(jnp.bfloat16).reshape(query_dims)


def per_device_plain(resid, spatial_q, spatial_k, spatial_v, out_weight, norm_gain, qkv_weight):
    context = spatial_attend(spatial_q, spatial_k, spatial_v)
    frames_here, clips_here, patches_all, heads_width = context.shape
    model_width = out_weight.shape[1]
    patch_major = context.transpose(2, 0, 1, 3)
    own_share = lax.psum_scatter(
        jnp.einsum(
            "pfcj,jd->pfcd", patch_major, out_weight, preferred_element_type=jnp.float32
        ).astype(jnp.bfloat16),
        "tensor",
        scatter_dimension=0,
        tiled=True,
    ).astype(jnp.float32)
    stream = resid.astype(jnp.float32) + own_share.transpose(1, 2, 0, 3)
    resid_out = stream.astype(jnp.bfloat16)
    normed = lax.all_gather(layer_norm(stream, norm_gain), "tensor", axis=2, tiled=True)
    flat_rows = normed.reshape(-1, model_width)
    qkv_width = 3 * qkv_weight.shape[2]
    block_rows = lax.all_gather(qkv_weight, "tm", axis=0, tiled=True)
    accumulated = jnp.dot(
        flat_rows,
        block_rows.reshape(block_rows.shape[0], qkv_width),
        preferred_element_type=jnp.float32,
    )
    projected = accumulated.astype(jnp.bfloat16).reshape(
        frames_here, clips_here, patches_all, 3, qkv_weight.shape[2]
    )
    exchanged = lax.all_to_all(projected, "tm", split_axis=2, concat_axis=0, tiled=True)
    patch_context = temporal_attend(
        exchanged[:, :, :, 0], exchanged[:, :, :, 1], exchanged[:, :, :, 2]
    )
    temporal_ctx = lax.all_to_all(patch_context, "tm", split_axis=0, concat_axis=2, tiled=True)
    return (resid_out, temporal_ctx)


def attend(queries, keys_in, values, same=None):
    scores = lax.dot_general(
        queries, keys_in, (((1,), (1,)), ((), ())), preferred_element_type=jnp.float32
    ) * (1.0 / math.sqrt(HD))
    if same is not None:
        scores = jnp.where(same, scores, -jnp.inf)
    top = jnp.max(scores, axis=1, keepdims=True)
    raised = jnp.exp(scores - top)
    total = jnp.sum(raised, axis=1, keepdims=True)
    probs = (raised * (1.0 / total)).astype(jnp.bfloat16)
    context = jnp.dot(probs, values, preferred_element_type=jnp.float32)
    return context.astype(jnp.bfloat16)


def spatial_kernel(heads, sides, rows, where, q_ref, k_ref, v_ref, keep_ref, send_ref, held):
    core = where[1]
    for head in range(heads):
        lanes = slice(head * HD, (head + 1) * HD)
        held[:, lanes] = attend(q_ref[0, 0, :, lanes], k_ref[0, 0, :, lanes], v_ref[0, 0, :, lanes])
    for side in range(sides):
        own = pl.multiple_of((side * 2 + core) * rows, rows)
        other = pl.multiple_of((side * 2 + 1 - core) * rows, rows)
        keep_ref[0, side] = held[pl.ds(own, rows), :]
        send_ref[0, side] = held[pl.ds(other, rows), :]


def spatial(where, spatial_q, spatial_k, spatial_v, clip_at, rows):
    frames, _, patches, width = spatial_q.shape
    sides = patches // (2 * rows)
    block = pl.BlockSpec((1, 1, patches, width), lambda f, w: (f, clip_at, 0, 0))
    half = pl.BlockSpec((1, sides, rows, width), lambda f, w: (f, 0, 0, 0))
    shape = jax.ShapeDtypeStruct((frames, sides, rows, width), jnp.bfloat16)
    heads = width // HD
    return pl.pallas_call(
        functools.partial(spatial_kernel, heads, sides, rows),
        grid_spec=pltpu.PrefetchScalarGridSpec(
            num_scalar_prefetch=1,
            grid=(frames,),
            in_specs=[block] * 3,
            out_specs=[half] * 2,
            scratch_shapes=[pltpu.VMEM((patches, width), jnp.bfloat16)],
        ),
        out_shape=[shape, shape],
        compiler_params=pltpu.CompilerParams(vmem_limit_bytes=32 * MIB),
        cost_estimate=pl.CostEstimate(
            flops=4 * frames * heads * patches * patches * HD,
            bytes_accessed=8 * frames * patches * width,
            transcendentals=frames * heads * patches * patches,
        ),
    )(where, spatial_q, spatial_k, spatial_v)


def branch_tile(keep_ref, came_ref, own_ref, other_ref):
    frames, _, rows, width = keep_ref.shape
    partial = jnp.dot(
        keep_ref[:, 0].reshape(frames * rows, width), own_ref[...],
        preferred_element_type=jnp.float32,
    )
    return partial + jnp.dot(
        came_ref[:, 0].reshape(frames * rows, width), other_ref[...],
        preferred_element_type=jnp.float32,
    )


def send_kernel(where, keep_ref, came_ref, own_ref, other_ref, out_ref):
    out_ref[...] = branch_tile(keep_ref, came_ref, own_ref, other_ref).astype(jnp.bfloat16)


def branch_cost(frames, rows, width, model):
    return pl.CostEstimate(
        flops=4 * frames * rows * width * model,
        bytes_accessed=4 * width * model + 8 * frames * rows * model,
        transcendentals=0,
    )


def branch_for_other(where, keep, came, own_weight, other_weight, tile):
    frames, _, rows, width = keep.shape
    model = own_weight.shape[1]
    context = pl.BlockSpec((frames, 1, rows, width), lambda n, w: (0, 1 - w[0], 0, 0))
    weight = pl.BlockSpec((width, tile), lambda n, w: (0, n))
    return pl.pallas_call(
        send_kernel,
        grid_spec=pltpu.PrefetchScalarGridSpec(
            num_scalar_prefetch=1,
            grid=(model // tile,),
            in_specs=[context, context, weight, weight],
            out_specs=pl.BlockSpec((frames * rows, tile), lambda n, w: (0, n)),
        ),
        out_shape=jax.ShapeDtypeStruct((frames * rows, model), jnp.bfloat16),
        compiler_params=pltpu.CompilerParams(vmem_limit_bytes=32 * MIB),
        cost_estimate=branch_cost(frames, rows, width, model),
    )(where, keep, came, own_weight, other_weight)


def norm_kernel(
    tiles, tile, ways, where, keep_ref, came_ref, own_ref, other_ref, branch_ref, resid_ref,
    gain_ref, *rest
):
    resid_out_ref, normed_refs, stream = rest[-ways - 2], rest[-ways - 1:-1], rest[-1]
    step = pl.program_id(0)
    frames, _, rows, _ = keep_ref.shape
    model = tiles * tile
    total = branch_tile(keep_ref, came_ref, own_ref, other_ref).astype(jnp.bfloat16)
    total = total.astype(jnp.float32) + branch_ref[...].astype(jnp.float32)
    total = total + resid_ref[:, 0].reshape(frames * rows, tile).astype(jnp.float32)
    resid_out_ref[:, 0] = total.astype(jnp.bfloat16).reshape(frames, rows, tile)
    stream[step] = total

    @pl.when(step == tiles - 1)
    def _():
        share = rows // ways
        for way in range(ways):
            goal = lax.rem(where[2] + way, ways)
            for frame in range(frames):
                at = pl.multiple_of(frame * rows + goal * share, share)
                picked = stream[:, pl.ds(at, share), :]
                average = jnp.sum(
                    jnp.sum(picked, axis=0), axis=-1, keepdims=True
                ) * (1.0 / model)
                centred = picked - average
                variance = jnp.sum(
                    jnp.sum(centred * centred, axis=0), axis=-1, keepdims=True
                ) * (1.0 / model)
                scale = lax.rsqrt(variance + 1e-06)
                for n in range(tiles):
                    lanes = slice(n * tile, (n + 1) * tile)
                    normed_refs[way][frame * share:(frame + 1) * share, lanes] = (
                        centred[n] * scale * gain_ref[:, lanes]
                    ).astype(jnp.bfloat16)


def norm(where, keep, came, own_weight, other_weight, branch, resid, gain, earlier, clip_at, tile, ways):
    frames, _, rows, width = keep.shape
    model = own_weight.shape[1]
    tiles = model // tile
    context = pl.BlockSpec((frames, 1, rows, width), lambda n, w: (0, w[0], 0, 0))
    weight = pl.BlockSpec((width, tile), lambda n, w: (0, n))
    residual = pl.BlockSpec((frames, 1, rows, tile), lambda n, w: (0, clip_at, 0, n))
    piece = (frames * rows // ways, model)
    return pl.pallas_call(
        functools.partial(norm_kernel, tiles, tile, ways),
        grid_spec=pltpu.PrefetchScalarGridSpec(
            num_scalar_prefetch=1,
            grid=(tiles,),
            in_specs=[
                context, context, weight, weight,
                pl.BlockSpec((frames * rows, tile), lambda n, w: (0, n)),
                residual,
                pl.BlockSpec((1, model), lambda n, w: (0, 0)),
            ] + [pl.BlockSpec(memory_space=pl.ANY)] * len(earlier),
            out_specs=[residual] + [pl.BlockSpec(piece, lambda n, w: (0, 0))] * ways,
            scratch_shapes=[pltpu.VMEM((tiles, frames * rows, tile), jnp.float32)],
        ),
        out_shape=[jax.ShapeDtypeStruct(resid.shape, jnp.bfloat16)]
        + [jax.ShapeDtypeStruct(piece, jnp.bfloat16)] * ways,
        input_output_aliases={8: 0} if earlier else {},
        compiler_params=pltpu.CompilerParams(vmem_limit_bytes=40 * MIB),
        cost_estimate=branch_cost(frames, rows, width, model),
    )(where, keep, came, own_weight, other_weight, branch, resid, gain, *earlier)


def project_kernel(steps, ways, share, piece_rows, where, *refs):
    pieces = refs[:steps * 2 * ways]
    at = steps * 2 * ways
    own_ref, near, far = refs[at], refs[at + 1:at + ways], refs[at + ways:at + 2 * ways - 1]
    outs = refs[at + 2 * ways - 1:at + 3 * ways - 1]
    rows_buf, weight_buf, qkv_buf, rows_sem, weight_sem = refs[at + 3 * ways - 1:]
    plane, home = where[3], where[2]
    half = near[0].shape[0]
    group = ways * piece_rows
    heads = qkv_buf.shape[2] // HD

    copies = [pltpu.make_async_copy(
        own_ref, weight_buf.at[pl.ds(pl.multiple_of(home * 2 * half, half), 2 * half)],
        weight_sem.at[0])]
    for way in range(1, ways):
        base = lax.rem(home + ways - way, ways) * 2 * half
        copies.append(pltpu.make_async_copy(
            near[way - 1],
            weight_buf.at[pl.ds(pl.multiple_of(base + plane * half, half), half)],
            weight_sem.at[2 * way - 1]))
        copies.append(pltpu.make_async_copy(
            far[way - 1],
            weight_buf.at[pl.ds(pl.multiple_of(base + (1 - plane) * half, half), half)],
            weight_sem.at[2 * way]))

    def row_copies(step):
        slot = step % 2
        return [pltpu.make_async_copy(
            pieces[step * 2 * ways + n],
            rows_buf.at[slot, pl.ds(n * piece_rows, piece_rows)],
            rows_sem.at[slot, n]) for n in range(2 * ways)]

    for copy in row_copies(0):
        copy.start()
    for copy in copies:
        copy.start()
    position_q = lax.broadcasted_iota(jnp.int32, (group, group), 0)
    position_k = lax.broadcasted_iota(jnp.int32, (group, group), 1)
    same = lax.rem(position_q, share) == lax.rem(position_k, share)

    def body(step, carry):
        slot = lax.rem(step, 2)
        for n in range(steps):
            @pl.when(step == n)
            def _():
                if n + 1 < steps:
                    for copy in row_copies(n + 1):
                        copy.start()
                for copy in row_copies(n):
                    copy.wait()
                if n == 0:
                    for copy in copies:
                        copy.wait()

        def column(part, carry):
            lanes = pl.ds(pl.multiple_of(part * heads * HD, heads * HD), heads * HD)
            qkv_buf[part] = jnp.dot(
                rows_buf[slot], weight_buf[:, lanes], preferred_element_type=jnp.float32
            ).astype(jnp.bfloat16)
            return carry

        lax.fori_loop(0, 3, column, 0)
        for which in range(2):
            rows = slice(which * group, (which + 1) * group)
            for head in range(heads):
                lanes = slice(head * HD, (head + 1) * HD)
                context = attend(
                    qkv_buf[0, rows, lanes], qkv_buf[1, rows, lanes], qkv_buf[2, rows, lanes], same
                )
                for way in range(ways):
                    outs[way][step * 2 + which, :, lanes] = context[
                        way * piece_rows:(way + 1) * piece_rows
                    ]
        return carry

    lax.fori_loop(0, steps, body, 0)


def project(where, pieces, own, near, far, ways, share):
    groups = len(pieces)
    steps = groups // 2
    piece_rows, model = pieces[0][0].shape
    width = own.shape[1] // 3
    flat = [piece for group in pieces for piece in group]
    rows = piece_rows * ways * groups
    out = (groups, piece_rows, width)
    return pl.pallas_call(
        functools.partial(project_kernel, steps, ways, share, piece_rows),
        grid_spec=pltpu.PrefetchScalarGridSpec(
            num_scalar_prefetch=1,
            grid=(1,),
            in_specs=[pl.BlockSpec(memory_space=pl.ANY)] * (len(flat) + 2 * ways - 1),
            out_specs=[pl.BlockSpec(out, lambda n, w: (0, 0, 0))] * ways,
            scratch_shapes=[
                pltpu.VMEM((2, 2 * ways * piece_rows, model), jnp.bfloat16),
                pltpu.VMEM((model, 3 * width), jnp.bfloat16),
                pltpu.VMEM((3, 2 * ways * piece_rows, width), jnp.bfloat16),
                pltpu.SemaphoreType.DMA((2, 2 * ways)),
                pltpu.SemaphoreType.DMA((2 * ways - 1,)),
            ],
        ),
        out_shape=[jax.ShapeDtypeStruct(out, jnp.bfloat16)] * ways,
        compiler_params=pltpu.CompilerParams(vmem_limit_bytes=48 * MIB),
        cost_estimate=pl.CostEstimate(
            flops=6 * rows * model * width,
            bytes_accessed=2 * rows * model + 6 * model * width,
            transcendentals=rows * ways * piece_rows,
        ),
    )(where, *flat, own, *near, *far)


def assemble_kernel(clips, sources, ways, groups, share, where, *refs):
    out_ref = refs[-1]
    width = refs[0].shape[-1]
    for clip in range(clips):
        for source in range(sources):
            side = where[0] if source % 2 == 0 else 1 - where[0]
            core = where[1] if source < 2 else 1 - where[1]
            for way in range(ways):
                origin = lax.rem(where[2] + ways - way, ways)
                row = pl.multiple_of(
                    ((side * 2 + core) * ways + origin) * share, share
                )
                for group in range(groups):
                    out_ref[0, clip, pl.ds(row, share), group * width:(group + 1) * width] = refs[
                        (clip * groups + group) * ways + way
                    ][source]


def assemble(where, arrived, frames, patches, share):
    clips, groups, ways = len(arrived), len(arrived[0]), len(arrived[0][0])
    flat = [array for clip in arrived for group in clip for array in group]
    sources, _, width = flat[0].shape
    return pl.pallas_call(
        functools.partial(assemble_kernel, clips, sources, ways, groups, share),
        grid_spec=pltpu.PrefetchScalarGridSpec(
            num_scalar_prefetch=1,
            grid=(frames,),
            in_specs=[pl.BlockSpec((sources, share, width), lambda f, w: (0, f, 0))] * len(flat),
            out_specs=pl.BlockSpec(
                (1, clips, patches, groups * width), lambda f, w: (f, 0, 0, 0)
            ),
        ),
        out_shape=jax.ShapeDtypeStruct((frames, clips, patches, groups * width), jnp.bfloat16),
        compiler_params=pltpu.CompilerParams(vmem_limit_bytes=32 * MIB),
    )(where, *flat)


def per_device(ways, resid, spatial_q, spatial_k, spatial_v, out_weight, norm_gain, qkv_weight):
    frames, clips, rows, model = resid.shape
    patches, width = spatial_q.shape[2:]
    share = rows // ways
    block = qkv_weight.shape[0]
    groups = 3
    tile = 1024

    plane, home, place = lax.axis_index("clip"), lax.axis_index("tm"), lax.axis_index("tensor")
    where = jnp.stack([place // 2, place % 2, home, plane]).astype(jnp.int32)

    def other_core(array):
        return lax.ppermute(array, "tensor", [(0, 1), (1, 0), (2, 3), (3, 2)])

    def other_side(array):
        return lax.ppermute(array, "tensor", [(0, 2), (2, 0), (1, 3), (3, 1)])

    def other_plane(array):
        return lax.ppermute(array, "clip", [(0, 1), (1, 0)])

    def along(array, way):
        return lax.ppermute(array, "tm", [(n, (n + way) % ways) for n in range(ways)])

    per_group = width // groups
    own, near, far = [], [], []
    for group in range(groups):
        columns = qkv_weight[:, :, group * per_group:(group + 1) * per_group].reshape(
            block, 3 * per_group
        )
        own.append(columns)
        travelling = lax.dynamic_slice_in_dim(columns, plane * (block // 2), block // 2, 0)
        near.append([])
        far.append([])
        for _ in range(1, ways):
            travelling = along(travelling, 1)
            near[-1].append(travelling)
            far[-1].append(other_plane(travelling))

    other_weight = other_core(out_weight)
    gain = norm_gain.reshape(1, model)

    written = []
    attended = []
    for clip in range(clips):
        keep, send = spatial(where, spatial_q, spatial_k, spatial_v, clip, rows)
        attended.append((keep, other_core(send)))
    branches = []
    for clip in range(clips):
        branches.append(other_side(
            branch_for_other(where, *attended[clip], out_weight, other_weight, tile)
        ))
    gathered = []
    for clip in range(clips):
        resid_out, *normed = norm(
            where, *attended[clip], out_weight, other_weight, branches[clip], resid, gain,
            written, clip, tile, ways,
        )
        written = [resid_out]
        mine = [normed[0]] + [along(normed[way], way) for way in range(1, ways)]
        beside = [other_side(piece) for piece in mine]
        gathered.append([
            mine, beside, [other_core(piece) for piece in mine],
            [other_core(piece) for piece in beside],
        ])

    arrived = [[None] * groups for _ in range(clips)]
    for group in range(groups):
        for clip in range(clips):
            contexts = project(
                where, gathered[clip], own[group], near[group], far[group], ways, share
            )
            arrived[clip][group] = [contexts[0]] + [
                along(contexts[way], ways - way) for way in range(1, ways)
            ]
    ordered = [
        [[got[0]] + [got[ways - way] for way in range(1, ways)] for got in by_group]
        for by_group in arrived
    ]
    temporal_ctx = assemble(where, ordered, frames, patches, share)
    return (resid_out, temporal_ctx)


def solution(mesh):
    placed = (
        P("tm", "clip", "tensor", None),
        P("tm", "clip", None, "tensor"),
        P("tm", "clip", None, "tensor"),
        P("tm", "clip", None, "tensor"),
        P("tensor", None),
        P(),
        P("tm", None, "tensor"),
    )
    small = mesh.shape["clip"] == 2 and mesh.shape["tm"] == 4 and mesh.shape["tensor"] == 4
    return jax.shard_map(
        functools.partial(per_device, mesh.shape["tm"]) if small else per_device_plain,
        mesh=mesh,
        in_specs=placed,
        out_specs=(P("tm", "clip", "tensor", None), P("tm", "clip", None, "tensor")),
        check_vma=False,
    )
```

```python
import functools
import math

import jax
import jax.numpy as jnp
from jax import lax
from jax.experimental import pallas as pl
from jax.experimental.pallas import tpu as pltpu
from jax.sharding import PartitionSpec as P

HD = 128
MIB = 1 << 20


def layer_norm(stream_in, norm_gain):
    average = jnp.mean(stream_in, axis=-1, keepdims=True)
    centred = stream_in - average
    variance = jnp.mean(centred * centred, axis=-1, keepdims=True)
    return (centred * lax.rsqrt(variance + 1e-06) * norm_gain).astype(jnp.bfloat16)


def spatial_attend(queries, keys_in, values):
    dims_in = queries.shape
    head_shape = dims_in[:3] + (dims_in[3] // HD, HD)
    query_heads = queries.reshape(head_shape)
    key_heads = keys_in.reshape(head_shape)
    value_heads = values.reshape(head_shape)
    scores = jnp.einsum(
        "fcphd,fcqhd->fchpq", query_heads, key_heads, preferred_element_type=jnp.float32
    ) / math.sqrt(HD)
    weights = jax.nn.softmax(scores, axis=-1).astype(jnp.bfloat16)
    context = jnp.einsum(
        "fchpq,fcqhd->fcphd", weights, value_heads, preferred_element_type=jnp.float32
    )
    return context.astype(jnp.bfloat16).reshape(dims_in)


def temporal_attend(queries, keys_in, values):
    query_dims = queries.shape
    heads_here = query_dims[3] // HD
    query_heads = queries.reshape(query_dims[:3] + (heads_here, HD))
    key_heads = keys_in.reshape(keys_in.shape[:3] + (heads_here, HD))
    value_heads = values.reshape(values.shape[:3] + (heads_here, HD))
    scores = jnp.einsum(
        "fcphd,gcphd->cphfg", query_heads, key_heads, preferred_element_type=jnp.float32
    ) / math.sqrt(HD)
    weights = jax.nn.softmax(scores, axis=-1).astype(jnp.bfloat16)
    context = jnp.einsum(
        "cphfg,gcphd->fcphd", weights, value_heads, preferred_element_type=jnp.float32
    )
    return context.astype(jnp.bfloat16).reshape(query_dims)


def per_device_plain(resid, spatial_q, spatial_k, spatial_v, out_weight, norm_gain, qkv_weight):
    context = spatial_attend(spatial_q, spatial_k, spatial_v)
    frames_here, clips_here, patches_all, heads_width = context.shape
    model_width = out_weight.shape[1]
    patch_major = context.transpose(2, 0, 1, 3)
    own_share = lax.psum_scatter(
        jnp.einsum(
            "pfcj,jd->pfcd", patch_major, out_weight, preferred_element_type=jnp.float32
        ).astype(jnp.bfloat16),
        "tensor",
        scatter_dimension=0,
        tiled=True,
    ).astype(jnp.float32)
    stream = resid.astype(jnp.float32) + own_share.transpose(1, 2, 0, 3)
    resid_out = stream.astype(jnp.bfloat16)
    normed = lax.all_gather(layer_norm(stream, norm_gain), "tensor", axis=2, tiled=True)
    flat_rows = normed.reshape(-1, model_width)
    qkv_width = 3 * qkv_weight.shape[2]
    block_rows = lax.all_gather(qkv_weight, "tm", axis=0, tiled=True)
    accumulated = jnp.dot(
        flat_rows,
        block_rows.reshape(block_rows.shape[0], qkv_width),
        preferred_element_type=jnp.float32,
    )
    projected = accumulated.astype(jnp.bfloat16).reshape(
        frames_here, clips_here, patches_all, 3, qkv_weight.shape[2]
    )
    exchanged = lax.all_to_all(projected, "tm", split_axis=2, concat_axis=0, tiled=True)
    patch_context = temporal_attend(
        exchanged[:, :, :, 0], exchanged[:, :, :, 1], exchanged[:, :, :, 2]
    )
    temporal_ctx = lax.all_to_all(patch_context, "tm", split_axis=0, concat_axis=2, tiled=True)
    return (resid_out, temporal_ctx)


def attend(queries, keys_in, values, same=None):
    scores = lax.dot_general(
        queries, keys_in, (((1,), (1,)), ((), ())), preferred_element_type=jnp.float32
    ) * (1.0 / math.sqrt(HD))
    if same is not None:
        scores = jnp.where(same, scores, -jnp.inf)
    top = jnp.max(scores, axis=1, keepdims=True)
    raised = jnp.exp(scores - top)
    total = jnp.sum(raised, axis=1, keepdims=True)
    probs = (raised * (1.0 / total)).astype(jnp.bfloat16)
    context = jnp.dot(probs, values, preferred_element_type=jnp.float32)
    return context.astype(jnp.bfloat16)


def spatial_kernel(heads, sides, rows, where, q_ref, k_ref, v_ref, *refs):
    keep_ref, send_ref, held = refs[-3:]
    core = where[1]
    for head in range(heads):
        lanes = slice(head * HD, (head + 1) * HD)
        held[:, lanes] = attend(q_ref[0, 0, :, lanes], k_ref[0, 0, :, lanes], v_ref[0, 0, :, lanes])
    for side in range(sides):
        own = pl.multiple_of((side * 2 + core) * rows, rows)
        other = pl.multiple_of((side * 2 + 1 - core) * rows, rows)
        keep_ref[0, side] = held[pl.ds(own, rows), :]
        send_ref[0, side] = held[pl.ds(other, rows), :]


def spatial(where, spatial_q, spatial_k, spatial_v, clip_at, rows, earlier):
    frames, _, patches, width = spatial_q.shape
    sides = patches // (2 * rows)
    block = pl.BlockSpec((1, 1, patches, width), lambda f, w: (f, clip_at, 0, 0))
    half = pl.BlockSpec((1, sides, rows, width), lambda f, w: (f, 0, 0, 0))
    shape = jax.ShapeDtypeStruct((frames, sides, rows, width), jnp.bfloat16)
    heads = width // HD
    return pl.pallas_call(
        functools.partial(spatial_kernel, heads, sides, rows),
        grid_spec=pltpu.PrefetchScalarGridSpec(
            num_scalar_prefetch=1,
            grid=(frames,),
            in_specs=[block] * 3 + [pl.BlockSpec(memory_space=pl.ANY)] * len(earlier),
            out_specs=[half] * 2,
            scratch_shapes=[pltpu.VMEM((patches, width), jnp.bfloat16)],
        ),
        out_shape=[shape, shape],
        compiler_params=pltpu.CompilerParams(vmem_limit_bytes=32 * MIB),
        cost_estimate=pl.CostEstimate(flops=0, bytes_accessed=0, transcendentals=0),
    )(where, spatial_q, spatial_k, spatial_v, *earlier)


def branch_tile(keep_ref, came_ref, own_ref, other_ref):
    frames, _, rows, width = keep_ref.shape
    partial = jnp.dot(
        keep_ref[:, 0].reshape(frames * rows, width), own_ref[...],
        preferred_element_type=jnp.float32,
    )
    return partial + jnp.dot(
        came_ref[:, 0].reshape(frames * rows, width), other_ref[...],
        preferred_element_type=jnp.float32,
    )


def send_kernel(where, keep_ref, came_ref, own_ref, other_ref, *refs):
    refs[-1][...] = branch_tile(keep_ref, came_ref, own_ref, other_ref).astype(jnp.bfloat16)


def branch_cost(frames, rows, width, model):
    return pl.CostEstimate(
        flops=4 * frames * rows * width * model,
        bytes_accessed=4 * width * model + 8 * frames * rows * model,
        transcendentals=0,
    )


def branch_for_other(where, keep, came, own_weight, other_weight, tile, earlier):
    frames, _, rows, width = keep.shape
    model = own_weight.shape[1]
    context = pl.BlockSpec((frames, 1, rows, width), lambda n, w: (0, 1 - w[0], 0, 0))
    weight = pl.BlockSpec((width, tile), lambda n, w: (0, n))
    return pl.pallas_call(
        send_kernel,
        grid_spec=pltpu.PrefetchScalarGridSpec(
            num_scalar_prefetch=1,
            grid=(model // tile,),
            in_specs=[context, context, weight, weight]
            + [pl.BlockSpec(memory_space=pl.ANY)] * len(earlier),
            out_specs=pl.BlockSpec((frames * rows, tile), lambda n, w: (0, n)),
        ),
        out_shape=jax.ShapeDtypeStruct((frames * rows, model), jnp.bfloat16),
        compiler_params=pltpu.CompilerParams(vmem_limit_bytes=32 * MIB),
        cost_estimate=pl.CostEstimate(flops=0, bytes_accessed=0, transcendentals=0),
    )(where, keep, came, own_weight, other_weight, *earlier)


def norm_kernel(
    tiles, tile, ways, where, keep_ref, came_ref, own_ref, other_ref, branch_ref, resid_ref,
    gain_ref, *rest
):
    resid_out_ref, normed_refs, stream = rest[-ways - 2], rest[-ways - 1:-1], rest[-1]
    step = pl.program_id(0)
    frames, _, rows, _ = keep_ref.shape
    model = tiles * tile
    total = branch_tile(keep_ref, came_ref, own_ref, other_ref).astype(jnp.bfloat16)
    total = total.astype(jnp.float32) + branch_ref[...].astype(jnp.float32)
    total = total + resid_ref[:, 0].reshape(frames * rows, tile).astype(jnp.float32)
    resid_out_ref[:, 0] = total.astype(jnp.bfloat16).reshape(frames, rows, tile)
    stream[step] = total

    @pl.when(step == tiles - 1)
    def _():
        share = rows // ways
        for way in range(ways):
            goal = lax.rem(where[2] + way, ways)
            for frame in range(frames):
                at = pl.multiple_of(frame * rows + goal * share, share)
                picked = stream[:, pl.ds(at, share), :]
                average = jnp.sum(
                    jnp.sum(picked, axis=0), axis=-1, keepdims=True
                ) * (1.0 / model)
                centred = picked - average
                variance = jnp.sum(
                    jnp.sum(centred * centred, axis=0), axis=-1, keepdims=True
                ) * (1.0 / model)
                scale = lax.rsqrt(variance + 1e-06)
                for n in range(tiles):
                    lanes = slice(n * tile, (n + 1) * tile)
                    normed_refs[way][frame * share:(frame + 1) * share, lanes] = (
                        centred[n] * scale * gain_ref[:, lanes]
                    ).astype(jnp.bfloat16)


def norm(where, keep, came, own_weight, other_weight, branch, resid, gain, written, clip_at, tile, ways, earlier):
    frames, _, rows, width = keep.shape
    model = own_weight.shape[1]
    tiles = model // tile
    context = pl.BlockSpec((frames, 1, rows, width), lambda n, w: (0, w[0], 0, 0))
    weight = pl.BlockSpec((width, tile), lambda n, w: (0, n))
    residual = pl.BlockSpec((frames, 1, rows, tile), lambda n, w: (0, clip_at, 0, n))
    piece = (frames * rows // ways, model)
    return pl.pallas_call(
        functools.partial(norm_kernel, tiles, tile, ways),
        grid_spec=pltpu.PrefetchScalarGridSpec(
            num_scalar_prefetch=1,
            grid=(tiles,),
            in_specs=[
                context, context, weight, weight,
                pl.BlockSpec((frames * rows, tile), lambda n, w: (0, n)),
                residual,
                pl.BlockSpec((1, model), lambda n, w: (0, 0)),
            ] + [pl.BlockSpec(memory_space=pl.ANY)] * (len(written) + len(earlier)),
            out_specs=[residual] + [pl.BlockSpec(piece, lambda n, w: (0, 0))] * ways,
            scratch_shapes=[pltpu.VMEM((tiles, frames * rows, tile), jnp.float32)],
        ),
        out_shape=[jax.ShapeDtypeStruct(resid.shape, jnp.bfloat16)]
        + [jax.ShapeDtypeStruct(piece, jnp.bfloat16)] * ways,
        input_output_aliases={8: 0} if written else {},
        compiler_params=pltpu.CompilerParams(vmem_limit_bytes=40 * MIB),
        cost_estimate=pl.CostEstimate(flops=0, bytes_accessed=0, transcendentals=0),
    )(where, keep, came, own_weight, other_weight, branch, resid, gain, *written, *earlier)


def project_kernel(steps, ways, share, piece_rows, part_at, where, *refs):
    pieces = refs[:steps * 2 * ways]
    at = steps * 2 * ways
    own_ref, near, far = refs[at], refs[at + 1:at + ways], refs[at + ways:at + 2 * ways - 1]
    outs = refs[-5 - ways:-5]
    rows_buf, weight_buf, qkv_buf, rows_sem, weight_sem = refs[-5:]
    plane, home = where[3], where[2]
    half = near[0].shape[0]
    group = ways * piece_rows
    heads = qkv_buf.shape[2] // HD

    width = heads * HD
    copies = [pltpu.make_async_copy(
        own_ref.at[part, :, part_at * width:(part_at + 1) * width],
        weight_buf.at[
            pl.ds(pl.multiple_of(home * 2 * half, half), 2 * half),
            part * width:(part + 1) * width,
        ],
        weight_sem.at[2 * ways - 2 + part]) for part in range(3)]
    for way in range(1, ways):
        base = lax.rem(home + ways - way, ways) * 2 * half
        copies.append(pltpu.make_async_copy(
            near[way - 1],
            weight_buf.at[pl.ds(pl.multiple_of(base + plane * half, half), half)],
            weight_sem.at[2 * way - 2]))
        copies.append(pltpu.make_async_copy(
            far[way - 1],
            weight_buf.at[pl.ds(pl.multiple_of(base + (1 - plane) * half, half), half)],
            weight_sem.at[2 * way - 1]))

    def row_copies(step):
        slot = step % 2
        return [pltpu.make_async_copy(
            pieces[step * 2 * ways + n],
            rows_buf.at[slot, pl.ds(n * piece_rows, piece_rows)],
            rows_sem.at[slot, n]) for n in range(2 * ways)]

    for copy in row_copies(0):
        copy.start()
    for copy in copies:
        copy.start()
    position_q = lax.broadcasted_iota(jnp.int32, (group, group), 0)
    position_k = lax.broadcasted_iota(jnp.int32, (group, group), 1)
    same = lax.rem(position_q, share) == lax.rem(position_k, share)

    def body(step, carry):
        slot = lax.rem(step, 2)
        for n in range(steps):
            @pl.when(step == n)
            def _():
                if n + 1 < steps:
                    for copy in row_copies(n + 1):
                        copy.start()
                for copy in row_copies(n):
                    copy.wait()
                if n == 0:
                    for copy in copies:
                        copy.wait()

        def column(part, carry):
            lanes = pl.ds(pl.multiple_of(part * heads * HD, heads * HD), heads * HD)
            qkv_buf[part] = jnp.dot(
                rows_buf[slot], weight_buf[:, lanes], preferred_element_type=jnp.float32
            ).astype(jnp.bfloat16)
            return carry

        lax.fori_loop(0, 3, column, 0)
        for which in range(2):
            rows = slice(which * group, (which + 1) * group)
            for head in range(heads):
                lanes = slice(head * HD, (head + 1) * HD)
                context = attend(
                    qkv_buf[0, rows, lanes], qkv_buf[1, rows, lanes], qkv_buf[2, rows, lanes], same
                )
                for way in range(ways):
                    outs[way][step * 2 + which, :, lanes] = context[
                        way * piece_rows:(way + 1) * piece_rows
                    ]
        return carry

    lax.fori_loop(0, steps, body, 0)


def project(where, pieces, weight, near, far, group, ways, share, earlier):
    groups = len(pieces)
    steps = groups // 2
    piece_rows, model = pieces[0][0].shape
    width = near[0].shape[1] // 3
    flat = [piece for group in pieces for piece in group]
    rows = piece_rows * ways * groups
    out = (groups, piece_rows, width)
    return pl.pallas_call(
        functools.partial(project_kernel, steps, ways, share, piece_rows, group),
        grid_spec=pltpu.PrefetchScalarGridSpec(
            num_scalar_prefetch=1,
            grid=(1,),
            in_specs=[pl.BlockSpec(memory_space=pl.ANY)] * (len(flat) + 2 * ways - 1 + len(earlier)),
            out_specs=[pl.BlockSpec(out, lambda n, w: (0, 0, 0))] * ways,
            scratch_shapes=[
                pltpu.VMEM((2, 2 * ways * piece_rows, model), jnp.bfloat16),
                pltpu.VMEM((model, 3 * width), jnp.bfloat16),
                pltpu.VMEM((3, 2 * ways * piece_rows, width), jnp.bfloat16),
                pltpu.SemaphoreType.DMA((2, 2 * ways)),
                pltpu.SemaphoreType.DMA((2 * ways + 1,)),
            ],
        ),
        out_shape=[jax.ShapeDtypeStruct(out, jnp.bfloat16)] * ways,
        compiler_params=pltpu.CompilerParams(vmem_limit_bytes=48 * MIB),
        cost_estimate=pl.CostEstimate(
            flops=6 * rows * model * width,
            bytes_accessed=2 * rows * model + 6 * model * width,
            transcendentals=rows * ways * piece_rows,
        ),
    )(where, *flat, weight, *near, *far, *earlier)


def assemble_kernel(clips, sources, ways, groups, share, where, *refs):
    out_ref = refs[-1]
    width = refs[0].shape[-1]
    for clip in range(clips):
        for source in range(sources):
            side = where[0] if source % 2 == 0 else 1 - where[0]
            core = where[1] if source < 2 else 1 - where[1]
            for way in range(ways):
                origin = lax.rem(where[2] + ways - way, ways)
                row = pl.multiple_of(
                    ((side * 2 + core) * ways + origin) * share, share
                )
                for group in range(groups):
                    out_ref[0, clip, pl.ds(row, share), group * width:(group + 1) * width] = refs[
                        (clip * groups + group) * ways + way
                    ][source]


def assemble(where, arrived, frames, patches, share):
    clips, groups, ways = len(arrived), len(arrived[0]), len(arrived[0][0])
    flat = [array for clip in arrived for group in clip for array in group]
    sources, _, width = flat[0].shape
    return pl.pallas_call(
        functools.partial(assemble_kernel, clips, sources, ways, groups, share),
        grid_spec=pltpu.PrefetchScalarGridSpec(
            num_scalar_prefetch=1,
            grid=(frames,),
            in_specs=[pl.BlockSpec((sources, share, width), lambda f, w: (0, f, 0))] * len(flat),
            out_specs=pl.BlockSpec(
                (1, clips, patches, groups * width), lambda f, w: (f, 0, 0, 0)
            ),
        ),
        out_shape=jax.ShapeDtypeStruct((frames, clips, patches, groups * width), jnp.bfloat16),
        compiler_params=pltpu.CompilerParams(vmem_limit_bytes=32 * MIB),
    )(where, *flat)


def passing_kernel(*refs):
    del refs


def after(arrays, *earlier):
    count = len(arrays)
    return list(pl.pallas_call(
        passing_kernel,
        in_specs=[pl.BlockSpec(memory_space=pl.ANY)] * (count + len(earlier)),
        out_specs=[pl.BlockSpec(memory_space=pl.ANY)] * count,
        out_shape=[jax.ShapeDtypeStruct(array.shape, array.dtype) for array in arrays],
        input_output_aliases={n: n for n in range(count)},
        cost_estimate=pl.CostEstimate(flops=0, bytes_accessed=0, transcendentals=0),
    )(*arrays, *earlier))


def columns_kernel(where, weight_ref, *refs):
    half_ref = refs[-1]
    width = weight_ref.shape[2]
    for part in range(3):
        half_ref[:, part * width:(part + 1) * width] = weight_ref[part]


def columns_of(where, weight, group, groups, earlier):
    _, block, width = weight.shape
    width = width // groups
    steps = 2
    rows = block // (2 * steps)
    return pl.pallas_call(
        columns_kernel,
        grid_spec=pltpu.PrefetchScalarGridSpec(
            num_scalar_prefetch=1,
            grid=(steps,),
            in_specs=[pl.BlockSpec((3, rows, width), lambda n, w: (0, n + steps * w[3], group))]
            + [pl.BlockSpec(memory_space=pl.ANY)] * len(earlier),
            out_specs=pl.BlockSpec((rows, 3 * width), lambda n, w: (n, 0)),
        ),
        out_shape=jax.ShapeDtypeStruct((block // 2, 3 * width), jnp.bfloat16),
        compiler_params=pltpu.CompilerParams(vmem_limit_bytes=32 * MIB),
        cost_estimate=pl.CostEstimate(flops=0, bytes_accessed=0, transcendentals=0),
    )(where, weight, *earlier)


def per_device(ways, resid, spatial_q, spatial_k, spatial_v, out_weight, norm_gain, qkv_weight):
    frames, clips, rows, model = resid.shape
    patches, width = spatial_q.shape[2:]
    share = rows // ways
    groups = 3
    tile = 1024

    plane, home, place = lax.axis_index("clip"), lax.axis_index("tm"), lax.axis_index("tensor")
    where = jnp.stack([place // 2, place % 2, home, plane]).astype(jnp.int32)

    def other_core(array):
        return lax.ppermute(array, "tensor", [(0, 1), (1, 0), (2, 3), (3, 2)])

    def other_side(array):
        return lax.ppermute(array, "tensor", [(0, 2), (2, 0), (1, 3), (3, 1)])

    def other_plane(array):
        return lax.ppermute(array, "clip", [(0, 1), (1, 0)])

    def along(array, way):
        return lax.ppermute(array, "tm", [(n, (n + way) % ways) for n in range(ways)])

    def norm_of(clip, written, *earlier):
        return norm(
            where, *attended[clip], out_weight, other_weight, branches[clip], resid, gain,
            written, clip, tile, ways, earlier,
        )

    weight = qkv_weight.transpose(1, 0, 2)
    gain = norm_gain.reshape(1, model)
    near = [[] for _ in range(groups)]
    far = [[] for _ in range(groups)]

    def pass_on(group, *earlier):
        (came,) = after([near[group][-1]], *earlier)
        near[group][-1] = came
        far[group].append(other_plane(came))
        if len(near[group]) < ways - 1:
            near[group].append(along(came, 1))
        return came

    other_weight = other_core(out_weight)
    start = [columns_of(where, weight, 0, groups, [])]
    near[0].append(along(start[0], 1))
    keep, send = spatial(where, spatial_q, spatial_k, spatial_v, 0, rows, [start[0]])
    attended = [(keep, other_core(send))]
    start.append(columns_of(where, weight, 1, groups, [send]))
    near[1].append(along(start[1], 1))
    first = branch_for_other(where, *attended[0], out_weight, other_weight, tile, [start[1]])
    branches = [other_side(first)]
    latest = pass_on(0, first)
    keep, send = spatial(where, spatial_q, spatial_k, spatial_v, 1, rows, [latest])
    attended.append((keep, other_core(send)))
    start.append(columns_of(where, weight, 2, groups, [send]))
    latest = pass_on(1, start[2])
    second = branch_for_other(where, *attended[1], out_weight, other_weight, tile, [latest])
    latest = pass_on(0, second)
    latest = pass_on(1, latest, far[0][0])
    (second,) = after([second], branches[0], latest)
    branches.append(other_side(second))
    resid_out, *normed = norm_of(0, [], second)
    mine = [[normed[0]] + [along(normed[way], way) for way in range(1, ways)]]
    latest = pass_on(0, normed[0], far[1][0])
    latest = pass_on(1, latest, far[0][1])
    resid_out, *normed = norm_of(1, [resid_out], latest)
    mine.append([normed[0]] + [along(normed[way], way) for way in range(1, ways)])
    mine[0][1:] = after(mine[0][1:], normed[0], far[1][1])
    beside = [[other_side(piece) for piece in mine[0]]]
    beside[0] = after(beside[0], mine[0][1], far[0][2])
    across = [[other_core(piece) for piece in mine[0] + beside[0]]]

    def project_of(clip, group, *earlier):
        pieces = [mine[clip], beside[clip], across[clip][:ways], across[clip][ways:]]
        return project(
            where, pieces, weight, near[group], far[group], group, ways, share, earlier
        )

    arrived = [[None] * groups for _ in range(clips)]

    def give_back(clip, group, contexts):
        arrived[clip][group] = [contexts[0]] + [
            along(contexts[way], ways - way) for way in range(1, ways)
        ]
        return contexts[0]

    *mine[1][1:], travelling = after(mine[1][1:] + [start[2]], beside[0][0], far[1][2])
    beside.append([other_side(piece) for piece in mine[1]])
    near[2].append(along(travelling, 1))
    latest = give_back(0, 0, project_of(0, 0, travelling))
    latest = pass_on(2, latest)
    latest = give_back(0, 1, project_of(0, 1, latest))
    latest = pass_on(2, latest)
    beside[1] = after(beside[1], latest)
    across.append([other_core(piece) for piece in mine[1] + beside[1]])
    latest = pass_on(2, beside[1][0], far[2][0])
    latest = give_back(1, 0, project_of(1, 0, latest))
    latest = give_back(1, 1, project_of(1, 1, latest))
    latest = give_back(0, 2, project_of(0, 2, latest))
    latest = give_back(1, 2, project_of(1, 2, latest))
    ordered = [
        [[got[0]] + [got[ways - way] for way in range(1, ways)] for got in by_group]
        for by_group in arrived
    ]
    temporal_ctx = assemble(where, ordered, frames, patches, share)
    return (resid_out, temporal_ctx)


def solution(mesh):
    placed = (
        P("tm", "clip", "tensor", None),
        P("tm", "clip", None, "tensor"),
        P("tm", "clip", None, "tensor"),
        P("tm", "clip", None, "tensor"),
        P("tensor", None),
        P(),
        P("tm", None, "tensor"),
    )
    small = mesh.shape["clip"] == 2 and mesh.shape["tm"] == 4 and mesh.shape["tensor"] == 4
    return jax.shard_map(
        functools.partial(per_device, mesh.shape["tm"]) if small else per_device_plain,
        mesh=mesh,
        in_specs=placed,
        out_specs=(P("tm", "clip", "tensor", None), P("tm", "clip", None, "tensor")),
        check_vma=False,
    )
```

```python
import functools
import math

import jax
import jax.numpy as jnp
from jax import lax
from jax.experimental import pallas as pl
from jax.experimental.pallas import tpu as pltpu
from jax.sharding import PartitionSpec as P

HD = 128
MIB = 1 << 20


def layer_norm(stream_in, norm_gain):
    average = jnp.mean(stream_in, axis=-1, keepdims=True)
    centred = stream_in - average
    variance = jnp.mean(centred * centred, axis=-1, keepdims=True)
    return (centred * lax.rsqrt(variance + 1e-06) * norm_gain).astype(jnp.bfloat16)


def spatial_attend(queries, keys_in, values):
    dims_in = queries.shape
    head_shape = dims_in[:3] + (dims_in[3] // HD, HD)
    query_heads = queries.reshape(head_shape)
    key_heads = keys_in.reshape(head_shape)
    value_heads = values.reshape(head_shape)
    scores = jnp.einsum(
        "fcphd,fcqhd->fchpq", query_heads, key_heads, preferred_element_type=jnp.float32
    ) / math.sqrt(HD)
    weights = jax.nn.softmax(scores, axis=-1).astype(jnp.bfloat16)
    context = jnp.einsum(
        "fchpq,fcqhd->fcphd", weights, value_heads, preferred_element_type=jnp.float32
    )
    return context.astype(jnp.bfloat16).reshape(dims_in)


def temporal_attend(queries, keys_in, values):
    query_dims = queries.shape
    heads_here = query_dims[3] // HD
    query_heads = queries.reshape(query_dims[:3] + (heads_here, HD))
    key_heads = keys_in.reshape(keys_in.shape[:3] + (heads_here, HD))
    value_heads = values.reshape(values.shape[:3] + (heads_here, HD))
    scores = jnp.einsum(
        "fcphd,gcphd->cphfg", query_heads, key_heads, preferred_element_type=jnp.float32
    ) / math.sqrt(HD)
    weights = jax.nn.softmax(scores, axis=-1).astype(jnp.bfloat16)
    context = jnp.einsum(
        "cphfg,gcphd->fcphd", weights, value_heads, preferred_element_type=jnp.float32
    )
    return context.astype(jnp.bfloat16).reshape(query_dims)


def per_device_plain(resid, spatial_q, spatial_k, spatial_v, out_weight, norm_gain, qkv_weight):
    context = spatial_attend(spatial_q, spatial_k, spatial_v)
    frames_here, clips_here, patches_all, heads_width = context.shape
    model_width = out_weight.shape[1]
    patch_major = context.transpose(2, 0, 1, 3)
    own_share = lax.psum_scatter(
        jnp.einsum(
            "pfcj,jd->pfcd", patch_major, out_weight, preferred_element_type=jnp.float32
        ).astype(jnp.bfloat16),
        "tensor",
        scatter_dimension=0,
        tiled=True,
    ).astype(jnp.float32)
    stream = resid.astype(jnp.float32) + own_share.transpose(1, 2, 0, 3)
    resid_out = stream.astype(jnp.bfloat16)
    normed = lax.all_gather(layer_norm(stream, norm_gain), "tensor", axis=2, tiled=True)
    flat_rows = normed.reshape(-1, model_width)
    qkv_width = 3 * qkv_weight.shape[2]
    block_rows = lax.all_gather(qkv_weight, "tm", axis=0, tiled=True)
    accumulated = jnp.dot(
        flat_rows,
        block_rows.reshape(block_rows.shape[0], qkv_width),
        preferred_element_type=jnp.float32,
    )
    projected = accumulated.astype(jnp.bfloat16).reshape(
        frames_here, clips_here, patches_all, 3, qkv_weight.shape[2]
    )
    exchanged = lax.all_to_all(projected, "tm", split_axis=2, concat_axis=0, tiled=True)
    patch_context = temporal_attend(
        exchanged[:, :, :, 0], exchanged[:, :, :, 1], exchanged[:, :, :, 2]
    )
    temporal_ctx = lax.all_to_all(patch_context, "tm", split_axis=0, concat_axis=2, tiled=True)
    return (resid_out, temporal_ctx)


def attend(queries, keys_in, values, same=None):
    scores = lax.dot_general(
        queries, keys_in, (((1,), (1,)), ((), ())), preferred_element_type=jnp.float32
    ) * (1.0 / math.sqrt(HD))
    if same is not None:
        scores = jnp.where(same, scores, -jnp.inf)
    top = jnp.max(scores, axis=1, keepdims=True)
    raised = jnp.exp(scores - top)
    total = jnp.sum(raised, axis=1, keepdims=True)
    probs = (raised * (1.0 / total)).astype(jnp.bfloat16)
    context = jnp.dot(probs, values, preferred_element_type=jnp.float32)
    return context.astype(jnp.bfloat16)


def spatial_kernel(heads, sides, rows, where, q_ref, k_ref, v_ref, *refs):
    keep_ref, send_ref, held = refs[-3:]
    core = where[1]
    for head in range(heads):
        lanes = slice(head * HD, (head + 1) * HD)
        held[:, lanes] = attend(q_ref[0, 0, :, lanes], k_ref[0, 0, :, lanes], v_ref[0, 0, :, lanes])
    for side in range(sides):
        own = pl.multiple_of((side * 2 + core) * rows, rows)
        other = pl.multiple_of((side * 2 + 1 - core) * rows, rows)
        keep_ref[0, side] = held[pl.ds(own, rows), :]
        send_ref[0, side] = held[pl.ds(other, rows), :]


def spatial(where, spatial_q, spatial_k, spatial_v, clip_at, rows, earlier):
    frames, _, patches, width = spatial_q.shape
    sides = patches // (2 * rows)
    block = pl.BlockSpec((1, 1, patches, width), lambda f, w: (f, clip_at, 0, 0))
    half = pl.BlockSpec((1, sides, rows, width), lambda f, w: (f, 0, 0, 0))
    shape = jax.ShapeDtypeStruct((frames, sides, rows, width), jnp.bfloat16)
    heads = width // HD
    return pl.pallas_call(
        functools.partial(spatial_kernel, heads, sides, rows),
        grid_spec=pltpu.PrefetchScalarGridSpec(
            num_scalar_prefetch=1,
            grid=(frames,),
            in_specs=[block] * 3 + [pl.BlockSpec(memory_space=pl.ANY)] * len(earlier),
            out_specs=[half] * 2,
            scratch_shapes=[pltpu.VMEM((patches, width), jnp.bfloat16)],
        ),
        out_shape=[shape, shape],
        compiler_params=pltpu.CompilerParams(vmem_limit_bytes=32 * MIB),
        cost_estimate=pl.CostEstimate(flops=0, bytes_accessed=0, transcendentals=0),
    )(where, spatial_q, spatial_k, spatial_v, *earlier)


def branch_tile(keep_ref, came_ref, own_ref, other_ref):
    frames, _, rows, width = keep_ref.shape
    partial = jnp.dot(
        keep_ref[:, 0].reshape(frames * rows, width), own_ref[...],
        preferred_element_type=jnp.float32,
    )
    return partial + jnp.dot(
        came_ref[:, 0].reshape(frames * rows, width), other_ref[...],
        preferred_element_type=jnp.float32,
    )


def send_kernel(where, keep_ref, came_ref, own_ref, other_ref, *refs):
    refs[-1][...] = branch_tile(keep_ref, came_ref, own_ref, other_ref).astype(jnp.bfloat16)


def branch_cost(frames, rows, width, model):
    return pl.CostEstimate(
        flops=4 * frames * rows * width * model,
        bytes_accessed=4 * width * model + 8 * frames * rows * model,
        transcendentals=0,
    )


def branch_for_other(where, keep, came, own_weight, other_weight, tile, earlier):
    frames, _, rows, width = keep.shape
    model = own_weight.shape[1]
    context = pl.BlockSpec((frames, 1, rows, width), lambda n, w: (0, 1 - w[0], 0, 0))
    weight = pl.BlockSpec((width, tile), lambda n, w: (0, n))
    return pl.pallas_call(
        send_kernel,
        grid_spec=pltpu.PrefetchScalarGridSpec(
            num_scalar_prefetch=1,
            grid=(model // tile,),
            in_specs=[context, context, weight, weight]
            + [pl.BlockSpec(memory_space=pl.ANY)] * len(earlier),
            out_specs=pl.BlockSpec((frames * rows, tile), lambda n, w: (0, n)),
        ),
        out_shape=jax.ShapeDtypeStruct((frames * rows, model), jnp.bfloat16),
        compiler_params=pltpu.CompilerParams(vmem_limit_bytes=32 * MIB),
        cost_estimate=pl.CostEstimate(flops=0, bytes_accessed=0, transcendentals=0),
    )(where, keep, came, own_weight, other_weight, *earlier)


def norm_kernel(
    tiles, tile, ways, where, keep_ref, came_ref, own_ref, other_ref, branch_ref, resid_ref,
    gain_ref, *rest
):
    resid_out_ref, normed_refs, stream = rest[-ways - 2], rest[-ways - 1:-1], rest[-1]
    step = pl.program_id(0)
    frames, _, rows, _ = keep_ref.shape
    model = tiles * tile
    total = branch_tile(keep_ref, came_ref, own_ref, other_ref).astype(jnp.bfloat16)
    total = total.astype(jnp.float32) + branch_ref[...].astype(jnp.float32)
    total = total + resid_ref[:, 0].reshape(frames * rows, tile).astype(jnp.float32)
    resid_out_ref[:, 0] = total.astype(jnp.bfloat16).reshape(frames, rows, tile)
    stream[step] = total

    @pl.when(step == tiles - 1)
    def _():
        share = rows // ways
        for way in range(ways):
            goal = lax.rem(where[2] + way, ways)
            for frame in range(frames):
                at = pl.multiple_of(frame * rows + goal * share, share)
                picked = stream[:, pl.ds(at, share), :]
                average = jnp.sum(
                    jnp.sum(picked, axis=0), axis=-1, keepdims=True
                ) * (1.0 / model)
                centred = picked - average
                variance = jnp.sum(
                    jnp.sum(centred * centred, axis=0), axis=-1, keepdims=True
                ) * (1.0 / model)
                scale = lax.rsqrt(variance + 1e-06)
                for n in range(tiles):
                    lanes = slice(n * tile, (n + 1) * tile)
                    normed_refs[way][frame * share:(frame + 1) * share, lanes] = (
                        centred[n] * scale * gain_ref[:, lanes]
                    ).astype(jnp.bfloat16)


def norm(where, keep, came, own_weight, other_weight, branch, resid, gain, written, clip_at, tile, ways, earlier):
    frames, _, rows, width = keep.shape
    model = own_weight.shape[1]
    tiles = model // tile
    context = pl.BlockSpec((frames, 1, rows, width), lambda n, w: (0, w[0], 0, 0))
    weight = pl.BlockSpec((width, tile), lambda n, w: (0, n))
    residual = pl.BlockSpec((frames, 1, rows, tile), lambda n, w: (0, clip_at, 0, n))
    piece = (frames * rows // ways, model)
    return pl.pallas_call(
        functools.partial(norm_kernel, tiles, tile, ways),
        grid_spec=pltpu.PrefetchScalarGridSpec(
            num_scalar_prefetch=1,
            grid=(tiles,),
            in_specs=[
                context, context, weight, weight,
                pl.BlockSpec((frames * rows, tile), lambda n, w: (0, n)),
                residual,
                pl.BlockSpec((1, model), lambda n, w: (0, 0)),
            ] + [pl.BlockSpec(memory_space=pl.ANY)] * (len(written) + len(earlier)),
            out_specs=[residual] + [pl.BlockSpec(piece, lambda n, w: (0, 0))] * ways,
            scratch_shapes=[pltpu.VMEM((tiles, frames * rows, tile), jnp.float32)],
        ),
        out_shape=[jax.ShapeDtypeStruct(resid.shape, jnp.bfloat16)]
        + [jax.ShapeDtypeStruct(piece, jnp.bfloat16)] * ways,
        input_output_aliases={8: 0} if written else {},
        compiler_params=pltpu.CompilerParams(vmem_limit_bytes=40 * MIB),
        cost_estimate=pl.CostEstimate(flops=0, bytes_accessed=0, transcendentals=0),
    )(where, keep, came, own_weight, other_weight, branch, resid, gain, *written, *earlier)


def project_kernel(steps, ways, share, places, block, other, where, *refs):
    pieces = refs[:steps * 2]
    own_ref, came = refs[steps * 2], refs[steps * 2 + 1:steps * 2 + 1 + len(places)]
    outs = refs[-5 - ways:-5]
    rows_buf, weight_buf, qkv_buf, rows_sem, weight_sem = refs[-5:]
    home = where[2]
    part_at = 1 - where[3] if other else where[3]
    group = pieces[0].shape[0]
    piece_rows = group // ways
    width = qkv_buf.shape[1] // 3
    heads = width // HD

    copies = [pltpu.make_async_copy(
        own_ref.at[part, :, pl.ds(pl.multiple_of(part_at * width, width), width)],
        weight_buf.at[
            pl.ds(pl.multiple_of(home * block, block), block),
            part * width:(part + 1) * width,
        ],
        weight_sem.at[len(places) + part]) for part in range(3)]
    for n, (way, first) in enumerate(places):
        rows = came[n].shape[0]
        base = pl.multiple_of(lax.rem(home + ways - way, ways) * block + first, rows)
        copies.append(pltpu.make_async_copy(
            came[n], weight_buf.at[pl.ds(base, rows)], weight_sem.at[n]))

    def row_copies(step):
        slot = step % 2
        return [pltpu.make_async_copy(
            pieces[step * 2 + n],
            rows_buf.at[slot, pl.ds(n * group, group)],
            rows_sem.at[slot, n]) for n in range(2)]

    for copy in row_copies(0):
        copy.start()
    for copy in copies:
        copy.start()
    position_q = lax.broadcasted_iota(jnp.int32, (group, group), 0)
    position_k = lax.broadcasted_iota(jnp.int32, (group, group), 1)
    same = lax.rem(position_q, share) == lax.rem(position_k, share)

    def body(step, carry):
        slot = lax.rem(step, 2)
        for n in range(steps):
            @pl.when(step == n)
            def _():
                if n + 1 < steps:
                    for copy in row_copies(n + 1):
                        copy.start()
                for copy in row_copies(n):
                    copy.wait()
                if n == 0:
                    for copy in copies:
                        copy.wait()

        qkv_buf[...] = jnp.dot(
            rows_buf[slot], weight_buf[...], preferred_element_type=jnp.float32
        ).astype(jnp.bfloat16)
        for which in range(2):
            rows = slice(which * group, (which + 1) * group)
            for head in range(heads):
                lanes = slice(head * HD, (head + 1) * HD)
                context = attend(*[
                    qkv_buf[rows, part * width + head * HD:part * width + (head + 1) * HD]
                    for part in range(3)
                ], same)
                for way in range(ways):
                    outs[way][step * 2 + which, :, lanes] = context[
                        way * piece_rows:(way + 1) * piece_rows
                    ]
        return carry

    lax.fori_loop(0, steps, body, 0)


def project(where, pieces, weight, came, other, ways, share, earlier):
    groups = len(pieces)
    steps = groups // 2
    rows, model = pieces[0].shape
    block = weight.shape[1]
    places = [(way, first) for way, first, _ in came]
    came = [array for _, _, array in came]
    width = came[0].shape[1] // 3
    out = (groups, rows // ways, width)
    return pl.pallas_call(
        functools.partial(project_kernel, steps, ways, share, places, block, other),
        grid_spec=pltpu.PrefetchScalarGridSpec(
            num_scalar_prefetch=1,
            grid=(1,),
            in_specs=[pl.BlockSpec(memory_space=pl.ANY)] * (groups + 1 + len(came) + len(earlier)),
            out_specs=[pl.BlockSpec(out, lambda n, w: (0, 0, 0))] * ways,
            scratch_shapes=[
                pltpu.VMEM((2, 2 * rows, model), jnp.bfloat16),
                pltpu.VMEM((model, 3 * width), jnp.bfloat16),
                pltpu.VMEM((2 * rows, 3 * width), jnp.bfloat16),
                pltpu.SemaphoreType.DMA((2, 2)),
                pltpu.SemaphoreType.DMA((len(came) + 3,)),
            ],
        ),
        out_shape=[jax.ShapeDtypeStruct(out, jnp.bfloat16)] * ways,
        compiler_params=pltpu.CompilerParams(vmem_limit_bytes=52 * MIB),
        cost_estimate=pl.CostEstimate(
            flops=6 * rows * groups * model * width,
            bytes_accessed=2 * rows * groups * model + 6 * model * width,
            transcendentals=rows * rows * groups * width // HD,
        ),
    )(where, *pieces, weight, *came, *earlier)


def assemble_kernel(clips, sources, ways, groups, share, where, *refs):
    out_ref = refs[-1]
    width = refs[0].shape[-1]
    for clip in range(clips):
        for source in range(sources):
            side = where[0] if source % 2 == 0 else 1 - where[0]
            core = where[1] if source < 2 else 1 - where[1]
            for way in range(ways):
                origin = lax.rem(where[2] + ways - way, ways)
                row = pl.multiple_of(
                    ((side * 2 + core) * ways + origin) * share, share
                )
                for group in range(groups):
                    part_at = where[3] if group == 0 else 1 - where[3]
                    lanes = pl.ds(pl.multiple_of(part_at * width, width), width)
                    out_ref[0, clip, pl.ds(row, share), lanes] = refs[
                        (clip * groups + group) * ways + way
                    ][source]


def assemble(where, arrived, frames, patches, share):
    clips, groups, ways = len(arrived), len(arrived[0]), len(arrived[0][0])
    flat = [array for clip in arrived for group in clip for array in group]
    sources, _, width = flat[0].shape
    return pl.pallas_call(
        functools.partial(assemble_kernel, clips, sources, ways, groups, share),
        grid_spec=pltpu.PrefetchScalarGridSpec(
            num_scalar_prefetch=1,
            grid=(frames,),
            in_specs=[pl.BlockSpec((sources, share, width), lambda f, w: (0, f, 0))] * len(flat),
            out_specs=pl.BlockSpec(
                (1, clips, patches, groups * width), lambda f, w: (f, 0, 0, 0)
            ),
        ),
        out_shape=jax.ShapeDtypeStruct((frames, clips, patches, groups * width), jnp.bfloat16),
        compiler_params=pltpu.CompilerParams(vmem_limit_bytes=32 * MIB),
    )(where, *flat)


def passing_kernel(*refs):
    del refs


def after(arrays, *earlier):
    count = len(arrays)
    return list(pl.pallas_call(
        passing_kernel,
        in_specs=[pl.BlockSpec(memory_space=pl.ANY)] * (count + len(earlier)),
        out_specs=[pl.BlockSpec(memory_space=pl.ANY)] * count,
        out_shape=[jax.ShapeDtypeStruct(array.shape, array.dtype) for array in arrays],
        input_output_aliases={n: n for n in range(count)},
        cost_estimate=pl.CostEstimate(flops=0, bytes_accessed=0, transcendentals=0),
    )(*arrays, *earlier))


def columns_kernel(where, weight_ref, *refs):
    half_ref = refs[-1]
    width = weight_ref.shape[2]
    for part in range(3):
        half_ref[:, part * width:(part + 1) * width] = weight_ref[part]


def columns_of(where, weight):
    _, block, width = weight.shape
    width = width // 2
    rows = block // 4
    return pl.pallas_call(
        columns_kernel,
        grid_spec=pltpu.PrefetchScalarGridSpec(
            num_scalar_prefetch=1,
            grid=(4,),
            in_specs=[pl.BlockSpec((3, rows, width), lambda n, w: (0, n, w[3]))],
            out_specs=pl.BlockSpec((rows, 3 * width), lambda n, w: (n, 0)),
        ),
        out_shape=jax.ShapeDtypeStruct((block, 3 * width), jnp.bfloat16),
        compiler_params=pltpu.CompilerParams(vmem_limit_bytes=32 * MIB),
        cost_estimate=pl.CostEstimate(flops=0, bytes_accessed=0, transcendentals=0),
    )(where, weight)


def join_kernel(ways, *refs):
    out_ref = refs[-1]
    rows = refs[0].shape[0]
    for way in range(ways):
        out_ref[way * rows:(way + 1) * rows] = refs[way][...]


def join(arrays, tile, *earlier):
    ways = len(arrays)
    rows, width = arrays[0].shape
    return pl.pallas_call(
        functools.partial(join_kernel, ways),
        grid=(width // tile,),
        in_specs=[pl.BlockSpec((rows, tile), lambda n: (0, n))] * ways
        + [pl.BlockSpec(memory_space=pl.ANY)] * len(earlier),
        out_specs=pl.BlockSpec((ways * rows, tile), lambda n: (0, n)),
        out_shape=jax.ShapeDtypeStruct((ways * rows, width), arrays[0].dtype),
        compiler_params=pltpu.CompilerParams(vmem_limit_bytes=32 * MIB),
        cost_estimate=pl.CostEstimate(flops=0, bytes_accessed=0, transcendentals=0),
    )(*arrays, *earlier)


def per_device(ways, resid, spatial_q, spatial_k, spatial_v, out_weight, norm_gain, qkv_weight):
    frames, clips, rows, model = resid.shape
    patches, width = spatial_q.shape[2:]
    share = rows // ways
    tile = 1024

    plane, home, place = lax.axis_index("clip"), lax.axis_index("tm"), lax.axis_index("tensor")
    where = jnp.stack([place // 2, place % 2, home, plane]).astype(jnp.int32)

    def other_core(array):
        return lax.ppermute(array, "tensor", [(0, 1), (1, 0), (2, 3), (3, 2)])

    def other_side(array):
        return lax.ppermute(array, "tensor", [(0, 2), (2, 0), (1, 3), (3, 1)])

    def other_plane(array):
        return lax.ppermute(array, "clip", [(0, 1), (1, 0)])

    def along(array, way):
        return lax.ppermute(array, "tm", [(n, (n + way) % ways) for n in range(ways)])

    def norm_of(clip, written, *earlier):
        return norm(
            where, *attended[clip], out_weight, other_weight, branches[clip], resid, gain,
            written, clip, tile, ways, earlier,
        )

    weight = qkv_weight.transpose(1, 0, 2)
    gain = norm_gain.reshape(1, model)
    near, far = [], []

    other_weight = other_core(out_weight)
    start = columns_of(where, weight)
    near.append(along(start, 1))
    keep, send = spatial(where, spatial_q, spatial_k, spatial_v, 0, rows, [start])
    attended = [(keep, other_core(send))]
    first = branch_for_other(where, *attended[0], out_weight, other_weight, tile, [])
    branches = [other_side(first)]
    keep, send = spatial(where, spatial_q, spatial_k, spatial_v, 1, rows, [first])
    attended.append((keep, other_core(send)))
    second = branch_for_other(where, *attended[1], out_weight, other_weight, tile, [])
    (near[0],) = after([near[0]], second)
    far.append(other_plane(near[0]))
    near.append(along(near[0], 1))
    (second,) = after([second], branches[0], near[0])
    branches.append(other_side(second))
    resid_out, *normed = norm_of(0, [], second)
    moved = [[normed[0]] + [along(normed[way], way) for way in range(1, ways)]]
    (near[1],) = after([near[1]], normed[0])
    far.append(other_plane(near[1]))
    resid_out, *normed = norm_of(1, [resid_out], near[1], far[0])
    moved.append([normed[0]] + [along(normed[way], way) for way in range(1, ways)])
    mine, beside, across = [], [], [None, None]

    def gather(clip, *earlier):
        mine.append(join(moved[clip], tile, *earlier))
        beside.append(other_side(mine[clip]))

    def project_of(clip, other, *earlier):
        pieces = [mine[clip], beside[clip], *across[clip]]
        arrays = far if other else near
        block = weight.shape[1]
        came = [(1, 0, arrays[0]), (2, 0, arrays[1]), (3, 0, arrays[2]), (3, block // 2, arrays[3])]
        return project(where, pieces, weight, came, other, ways, share, earlier)

    arrived = [[], []]

    def give_back(clip, contexts, *earlier):
        leaving = after(contexts[1:], *earlier) if earlier else contexts[1:]
        arrived[clip].append([contexts[0]] + [
            along(leaving[way - 1], ways - way) for way in range(1, ways)
        ])
        return contexts[0]

    gather(0, normed[0])
    gather(1, beside[0])
    half = weight.shape[1] // 2
    mine[0], beside[0], near[1] = after([mine[0], beside[0], near[1]], mine[1], far[1])
    near.append(along(near[1][:half], 1))
    near.append(along(near[1][half:], 1))
    across[0] = [other_core(mine[0]), other_core(beside[0])]
    (near[2],) = after([near[2]], *across[0])
    far.append(other_plane(near[2]))
    mine[1], beside[1], near[3] = after([mine[1], beside[1], near[3]], near[2])
    across[1] = [other_core(mine[1]), other_core(beside[1])]
    far.append(other_plane(near[3]))
    latest = give_back(0, project_of(0, False, near[3]))
    latest = give_back(1, project_of(1, False, latest), *arrived[0][0])
    latest = give_back(0, project_of(0, True, latest), *arrived[1][0])
    latest = give_back(1, project_of(1, True, latest), *arrived[0][1])
    ordered = [
        [[got[0]] + [got[ways - way] for way in range(1, ways)] for got in by_group]
        for by_group in arrived
    ]
    temporal_ctx = assemble(where, ordered, frames, patches, share)
    return (resid_out, temporal_ctx)


def solution(mesh):
    placed = (
        P("tm", "clip", "tensor", None),
        P("tm", "clip", None, "tensor"),
        P("tm", "clip", None, "tensor"),
        P("tm", "clip", None, "tensor"),
        P("tensor", None),
        P(),
        P("tm", None, "tensor"),
    )
    small = mesh.shape["clip"] == 2 and mesh.shape["tm"] == 4 and mesh.shape["tensor"] == 4
    return jax.shard_map(
        functools.partial(per_device, mesh.shape["tm"]) if small else per_device_plain,
        mesh=mesh,
        in_specs=placed,
        out_specs=(P("tm", "clip", "tensor", None), P("tm", "clip", None, "tensor")),
        check_vma=False,
    )
```

```python
import functools
import math

import jax
import jax.numpy as jnp
from jax import lax
from jax.experimental import pallas as pl
from jax.experimental.pallas import tpu as pltpu
from jax.sharding import PartitionSpec as P

HD = 128
MIB = 1 << 20


def layer_norm(stream_in, norm_gain):
    average = jnp.mean(stream_in, axis=-1, keepdims=True)
    centred = stream_in - average
    variance = jnp.mean(centred * centred, axis=-1, keepdims=True)
    return (centred * lax.rsqrt(variance + 1e-06) * norm_gain).astype(jnp.bfloat16)


def spatial_attend(queries, keys_in, values):
    dims_in = queries.shape
    head_shape = dims_in[:3] + (dims_in[3] // HD, HD)
    query_heads = queries.reshape(head_shape)
    key_heads = keys_in.reshape(head_shape)
    value_heads = values.reshape(head_shape)
    scores = jnp.einsum(
        "fcphd,fcqhd->fchpq", query_heads, key_heads, preferred_element_type=jnp.float32
    ) / math.sqrt(HD)
    weights = jax.nn.softmax(scores, axis=-1).astype(jnp.bfloat16)
    context = jnp.einsum(
        "fchpq,fcqhd->fcphd", weights, value_heads, preferred_element_type=jnp.float32
    )
    return context.astype(jnp.bfloat16).reshape(dims_in)


def temporal_attend(queries, keys_in, values):
    query_dims = queries.shape
    heads_here = query_dims[3] // HD
    query_heads = queries.reshape(query_dims[:3] + (heads_here, HD))
    key_heads = keys_in.reshape(keys_in.shape[:3] + (heads_here, HD))
    value_heads = values.reshape(values.shape[:3] + (heads_here, HD))
    scores = jnp.einsum(
        "fcphd,gcphd->cphfg", query_heads, key_heads, preferred_element_type=jnp.float32
    ) / math.sqrt(HD)
    weights = jax.nn.softmax(scores, axis=-1).astype(jnp.bfloat16)
    context = jnp.einsum(
        "cphfg,gcphd->fcphd", weights, value_heads, preferred_element_type=jnp.float32
    )
    return context.astype(jnp.bfloat16).reshape(query_dims)


def per_device_plain(resid, spatial_q, spatial_k, spatial_v, out_weight, norm_gain, qkv_weight):
    context = spatial_attend(spatial_q, spatial_k, spatial_v)
    frames_here, clips_here, patches_all, heads_width = context.shape
    model_width = out_weight.shape[1]
    patch_major = context.transpose(2, 0, 1, 3)
    own_share = lax.psum_scatter(
        jnp.einsum(
            "pfcj,jd->pfcd", patch_major, out_weight, preferred_element_type=jnp.float32
        ).astype(jnp.bfloat16),
        "tensor",
        scatter_dimension=0,
        tiled=True,
    ).astype(jnp.float32)
    stream = resid.astype(jnp.float32) + own_share.transpose(1, 2, 0, 3)
    resid_out = stream.astype(jnp.bfloat16)
    normed = lax.all_gather(layer_norm(stream, norm_gain), "tensor", axis=2, tiled=True)
    flat_rows = normed.reshape(-1, model_width)
    qkv_width = 3 * qkv_weight.shape[2]
    block_rows = lax.all_gather(qkv_weight, "tm", axis=0, tiled=True)
    accumulated = jnp.dot(
        flat_rows,
        block_rows.reshape(block_rows.shape[0], qkv_width),
        preferred_element_type=jnp.float32,
    )
    projected = accumulated.astype(jnp.bfloat16).reshape(
        frames_here, clips_here, patches_all, 3, qkv_weight.shape[2]
    )
    exchanged = lax.all_to_all(projected, "tm", split_axis=2, concat_axis=0, tiled=True)
    patch_context = temporal_attend(
        exchanged[:, :, :, 0], exchanged[:, :, :, 1], exchanged[:, :, :, 2]
    )
    temporal_ctx = lax.all_to_all(patch_context, "tm", split_axis=0, concat_axis=2, tiled=True)
    return (resid_out, temporal_ctx)


def attend(queries, keys_in, values, same=None):
    scores = lax.dot_general(
        queries, keys_in, (((1,), (1,)), ((), ())), preferred_element_type=jnp.float32
    ) * (1.0 / math.sqrt(HD))
    if same is not None:
        scores = jnp.where(same, scores, -jnp.inf)
    top = jnp.max(scores, axis=1, keepdims=True)
    raised = jnp.exp(scores - top)
    summed = jnp.concatenate([values, jnp.ones_like(values)], axis=1)
    context = jnp.dot(raised.astype(jnp.bfloat16), summed, preferred_element_type=jnp.float32)
    return (context[:, :HD] / context[:, HD:]).astype(jnp.bfloat16)


def spatial_kernel(heads, sides, rows, where, q_ref, k_ref, v_ref, *refs):
    keep_ref, send_ref, held = refs[-3:]
    core = where[1]
    for head in range(heads):
        lanes = slice(head * HD, (head + 1) * HD)
        held[:, lanes] = attend(q_ref[0, 0, :, lanes], k_ref[0, 0, :, lanes], v_ref[0, 0, :, lanes])
    for side in range(sides):
        own = pl.multiple_of((side * 2 + core) * rows, rows)
        other = pl.multiple_of((side * 2 + 1 - core) * rows, rows)
        keep_ref[0, side] = held[pl.ds(own, rows), :]
        send_ref[0, side] = held[pl.ds(other, rows), :]


def spatial(where, spatial_q, spatial_k, spatial_v, clip_at, rows, earlier):
    frames, _, patches, width = spatial_q.shape
    sides = patches // (2 * rows)
    block = pl.BlockSpec((1, 1, patches, width), lambda f, w: (f, clip_at, 0, 0))
    half = pl.BlockSpec((1, sides, rows, width), lambda f, w: (f, 0, 0, 0))
    shape = jax.ShapeDtypeStruct((frames, sides, rows, width), jnp.bfloat16)
    heads = width // HD
    return pl.pallas_call(
        functools.partial(spatial_kernel, heads, sides, rows),
        grid_spec=pltpu.PrefetchScalarGridSpec(
            num_scalar_prefetch=1,
            grid=(frames,),
            in_specs=[block] * 3 + [pl.BlockSpec(memory_space=pl.ANY)] * len(earlier),
            out_specs=[half] * 2,
            scratch_shapes=[pltpu.VMEM((patches, width), jnp.bfloat16)],
        ),
        out_shape=[shape, shape],
        compiler_params=pltpu.CompilerParams(vmem_limit_bytes=32 * MIB),
        cost_estimate=pl.CostEstimate(flops=0, bytes_accessed=0, transcendentals=0),
    )(where, spatial_q, spatial_k, spatial_v, *earlier)


def branch_tile(keep_ref, came_ref, own_ref, other_ref):
    frames, _, rows, width = keep_ref.shape
    partial = jnp.dot(
        keep_ref[:, 0].reshape(frames * rows, width), own_ref[...],
        preferred_element_type=jnp.float32,
    )
    return partial + jnp.dot(
        came_ref[:, 0].reshape(frames * rows, width), other_ref[...],
        preferred_element_type=jnp.float32,
    )


def send_kernel(where, keep_ref, came_ref, own_ref, other_ref, *refs):
    refs[-1][...] = branch_tile(keep_ref, came_ref, own_ref, other_ref).astype(jnp.bfloat16)


def branch_cost(frames, rows, width, model):
    return pl.CostEstimate(
        flops=4 * frames * rows * width * model,
        bytes_accessed=4 * width * model + 8 * frames * rows * model,
        transcendentals=0,
    )


def branch_for_other(where, keep, came, own_weight, other_weight, tile, earlier):
    frames, _, rows, width = keep.shape
    model = own_weight.shape[1]
    context = pl.BlockSpec((frames, 1, rows, width), lambda n, w: (0, 1 - w[0], 0, 0))
    weight = pl.BlockSpec((width, tile), lambda n, w: (0, n))
    return pl.pallas_call(
        send_kernel,
        grid_spec=pltpu.PrefetchScalarGridSpec(
            num_scalar_prefetch=1,
            grid=(model // tile,),
            in_specs=[context, context, weight, weight]
            + [pl.BlockSpec(memory_space=pl.ANY)] * len(earlier),
            out_specs=pl.BlockSpec((frames * rows, tile), lambda n, w: (0, n)),
        ),
        out_shape=jax.ShapeDtypeStruct((frames * rows, model), jnp.bfloat16),
        compiler_params=pltpu.CompilerParams(vmem_limit_bytes=32 * MIB),
        cost_estimate=pl.CostEstimate(flops=0, bytes_accessed=0, transcendentals=0),
    )(where, keep, came, own_weight, other_weight, *earlier)


def norm_kernel(
    tiles, tile, ways, where, keep_ref, came_ref, own_ref, other_ref, branch_ref, resid_ref,
    gain_ref, *rest
):
    resid_out_ref, normed_refs, stream = rest[-ways - 2], rest[-ways - 1:-1], rest[-1]
    step = pl.program_id(0)
    frames, _, rows, _ = keep_ref.shape
    model = tiles * tile
    total = branch_tile(keep_ref, came_ref, own_ref, other_ref).astype(jnp.bfloat16)
    total = total.astype(jnp.float32) + branch_ref[...].astype(jnp.float32)
    total = total + resid_ref[:, 0].reshape(frames * rows, tile).astype(jnp.float32)
    resid_out_ref[:, 0] = total.astype(jnp.bfloat16).reshape(frames, rows, tile)
    stream[step] = total

    @pl.when(step == tiles - 1)
    def _():
        share = rows // ways
        for way in range(ways):
            goal = lax.rem(where[2] + way, ways)
            for frame in range(frames):
                at = pl.multiple_of(frame * rows + goal * share, share)
                picked = stream[:, pl.ds(at, share), :]
                average = jnp.sum(
                    jnp.sum(picked, axis=0), axis=-1, keepdims=True
                ) * (1.0 / model)
                centred = picked - average
                variance = jnp.sum(
                    jnp.sum(centred * centred, axis=0), axis=-1, keepdims=True
                ) * (1.0 / model)
                scale = lax.rsqrt(variance + 1e-06)
                for n in range(tiles):
                    lanes = slice(n * tile, (n + 1) * tile)
                    normed_refs[way][frame * share:(frame + 1) * share, lanes] = (
                        centred[n] * scale * gain_ref[:, lanes]
                    ).astype(jnp.bfloat16)


def norm(where, keep, came, own_weight, other_weight, branch, resid, gain, written, clip_at, tile, ways, earlier):
    frames, _, rows, width = keep.shape
    model = own_weight.shape[1]
    tiles = model // tile
    context = pl.BlockSpec((frames, 1, rows, width), lambda n, w: (0, w[0], 0, 0))
    weight = pl.BlockSpec((width, tile), lambda n, w: (0, n))
    residual = pl.BlockSpec((frames, 1, rows, tile), lambda n, w: (0, clip_at, 0, n))
    piece = (frames * rows // ways, model)
    return pl.pallas_call(
        functools.partial(norm_kernel, tiles, tile, ways),
        grid_spec=pltpu.PrefetchScalarGridSpec(
            num_scalar_prefetch=1,
            grid=(tiles,),
            in_specs=[
                context, context, weight, weight,
                pl.BlockSpec((frames * rows, tile), lambda n, w: (0, n)),
                residual,
                pl.BlockSpec((1, model), lambda n, w: (0, 0)),
            ] + [pl.BlockSpec(memory_space=pl.ANY)] * (len(written) + len(earlier)),
            out_specs=[residual] + [pl.BlockSpec(piece, lambda n, w: (0, 0))] * ways,
            scratch_shapes=[pltpu.VMEM((tiles, frames * rows, tile), jnp.float32)],
        ),
        out_shape=[jax.ShapeDtypeStruct(resid.shape, jnp.bfloat16)]
        + [jax.ShapeDtypeStruct(piece, jnp.bfloat16)] * ways,
        input_output_aliases={8: 0} if written else {},
        compiler_params=pltpu.CompilerParams(vmem_limit_bytes=40 * MIB),
        cost_estimate=pl.CostEstimate(flops=0, bytes_accessed=0, transcendentals=0),
    )(where, keep, came, own_weight, other_weight, branch, resid, gain, *written, *earlier)


def project_kernel(steps, ways, share, places, block, other, where, *refs):
    pieces = refs[:steps * 2]
    own_ref, came = refs[steps * 2], refs[steps * 2 + 1:steps * 2 + 1 + len(places)]
    outs = refs[-5 - ways:-5]
    rows_buf, weight_buf, qkv_buf, rows_sem, weight_sem = refs[-5:]
    home = where[2]
    part_at = 1 - where[3] if other else where[3]
    group = pieces[0].shape[0]
    piece_rows = group // ways
    width = qkv_buf.shape[1] // 3
    heads = width // HD

    copies = [pltpu.make_async_copy(
        own_ref.at[part, :, pl.ds(pl.multiple_of(part_at * width, width), width)],
        weight_buf.at[
            pl.ds(pl.multiple_of(home * block, block), block),
            part * width:(part + 1) * width,
        ],
        weight_sem.at[len(places) + part]) for part in range(3)]
    for n, (way, first) in enumerate(places):
        rows = came[n].shape[0]
        base = pl.multiple_of(lax.rem(home + ways - way, ways) * block + first, rows)
        copies.append(pltpu.make_async_copy(
            came[n], weight_buf.at[pl.ds(base, rows)], weight_sem.at[n]))

    def row_copies(step):
        slot = step % 2
        return [pltpu.make_async_copy(
            pieces[step * 2 + n],
            rows_buf.at[slot, pl.ds(n * group, group)],
            rows_sem.at[slot, n]) for n in range(2)]

    for copy in row_copies(0):
        copy.start()
    for copy in copies:
        copy.start()
    position_q = lax.broadcasted_iota(jnp.int32, (group, group), 0)
    position_k = lax.broadcasted_iota(jnp.int32, (group, group), 1)
    same = lax.rem(position_q, share) == lax.rem(position_k, share)

    def body(step, carry):
        slot = lax.rem(step, 2)
        for n in range(steps):
            @pl.when(step == n)
            def _():
                if n + 1 < steps:
                    for copy in row_copies(n + 1):
                        copy.start()
                for copy in row_copies(n):
                    copy.wait()
                if n == 0:
                    for copy in copies:
                        copy.wait()

        qkv_buf[...] = jnp.dot(
            rows_buf[slot], weight_buf[...], preferred_element_type=jnp.float32
        ).astype(jnp.bfloat16)
        for which in range(2):
            rows = slice(which * group, (which + 1) * group)
            for head in range(heads):
                lanes = slice(head * HD, (head + 1) * HD)
                context = attend(*[
                    qkv_buf[rows, part * width + head * HD:part * width + (head + 1) * HD]
                    for part in range(3)
                ], same)
                for way in range(ways):
                    outs[way][step * 2 + which, :, lanes] = context[
                        way * piece_rows:(way + 1) * piece_rows
                    ]
        return carry

    lax.fori_loop(0, steps, body, 0)


def project(where, pieces, weight, came, other, ways, share, earlier):
    groups = len(pieces)
    steps = groups // 2
    rows, model = pieces[0].shape
    block = weight.shape[1]
    places = [(way, first) for way, first, _ in came]
    came = [array for _, _, array in came]
    width = came[0].shape[1] // 3
    out = (groups, rows // ways, width)
    return pl.pallas_call(
        functools.partial(project_kernel, steps, ways, share, places, block, other),
        grid_spec=pltpu.PrefetchScalarGridSpec(
            num_scalar_prefetch=1,
            grid=(1,),
            in_specs=[pl.BlockSpec(memory_space=pl.ANY)] * (groups + 1 + len(came) + len(earlier)),
            out_specs=[pl.BlockSpec(out, lambda n, w: (0, 0, 0))] * ways,
            scratch_shapes=[
                pltpu.VMEM((2, 2 * rows, model), jnp.bfloat16),
                pltpu.VMEM((model, 3 * width), jnp.bfloat16),
                pltpu.VMEM((2 * rows, 3 * width), jnp.bfloat16),
                pltpu.SemaphoreType.DMA((2, 2)),
                pltpu.SemaphoreType.DMA((len(came) + 3,)),
            ],
        ),
        out_shape=[jax.ShapeDtypeStruct(out, jnp.bfloat16)] * ways,
        compiler_params=pltpu.CompilerParams(vmem_limit_bytes=52 * MIB),
        cost_estimate=pl.CostEstimate(
            flops=6 * rows * groups * model * width,
            bytes_accessed=2 * rows * groups * model + 6 * model * width,
            transcendentals=rows * rows * groups * width // HD,
        ),
    )(where, *pieces, weight, *came, *earlier)


def assemble_kernel(clips, sources, ways, groups, share, where, *refs):
    out_ref = refs[-1]
    width = refs[0].shape[-1]
    for clip in range(clips):
        for source in range(sources):
            side = where[0] if source % 2 == 0 else 1 - where[0]
            core = where[1] if source < 2 else 1 - where[1]
            for way in range(ways):
                origin = lax.rem(where[2] + ways - way, ways)
                row = pl.multiple_of(
                    ((side * 2 + core) * ways + origin) * share, share
                )
                for group in range(groups):
                    part_at = where[3] if group == 0 else 1 - where[3]
                    lanes = pl.ds(pl.multiple_of(part_at * width, width), width)
                    out_ref[0, clip, pl.ds(row, share), lanes] = refs[
                        (clip * groups + group) * ways + way
                    ][source]


def assemble(where, arrived, frames, patches, share):
    clips, groups, ways = len(arrived), len(arrived[0]), len(arrived[0][0])
    flat = [array for clip in arrived for group in clip for array in group]
    sources, _, width = flat[0].shape
    return pl.pallas_call(
        functools.partial(assemble_kernel, clips, sources, ways, groups, share),
        grid_spec=pltpu.PrefetchScalarGridSpec(
            num_scalar_prefetch=1,
            grid=(frames,),
            in_specs=[pl.BlockSpec((sources, share, width), lambda f, w: (0, f, 0))] * len(flat),
            out_specs=pl.BlockSpec(
                (1, clips, patches, groups * width), lambda f, w: (f, 0, 0, 0)
            ),
        ),
        out_shape=jax.ShapeDtypeStruct((frames, clips, patches, groups * width), jnp.bfloat16),
        compiler_params=pltpu.CompilerParams(vmem_limit_bytes=32 * MIB),
    )(where, *flat)


def passing_kernel(*refs):
    del refs


def after(arrays, *earlier):
    count = len(arrays)
    return list(pl.pallas_call(
        passing_kernel,
        in_specs=[pl.BlockSpec(memory_space=pl.ANY)] * (count + len(earlier)),
        out_specs=[pl.BlockSpec(memory_space=pl.ANY)] * count,
        out_shape=[jax.ShapeDtypeStruct(array.shape, array.dtype) for array in arrays],
        input_output_aliases={n: n for n in range(count)},
        cost_estimate=pl.CostEstimate(flops=0, bytes_accessed=0, transcendentals=0),
    )(*arrays, *earlier))


def columns_kernel(where, weight_ref, *refs):
    half_ref = refs[-1]
    width = weight_ref.shape[2]
    for part in range(3):
        half_ref[:, part * width:(part + 1) * width] = weight_ref[part]


def columns_of(where, weight):
    _, block, width = weight.shape
    width = width // 2
    rows = block // 4
    return pl.pallas_call(
        columns_kernel,
        grid_spec=pltpu.PrefetchScalarGridSpec(
            num_scalar_prefetch=1,
            grid=(4,),
            in_specs=[pl.BlockSpec((3, rows, width), lambda n, w: (0, n, w[3]))],
            out_specs=pl.BlockSpec((rows, 3 * width), lambda n, w: (n, 0)),
        ),
        out_shape=jax.ShapeDtypeStruct((block, 3 * width), jnp.bfloat16),
        compiler_params=pltpu.CompilerParams(vmem_limit_bytes=32 * MIB),
        cost_estimate=pl.CostEstimate(flops=0, bytes_accessed=0, transcendentals=0),
    )(where, weight)


def join_kernel(ways, *refs):
    out_ref = refs[-1]
    rows = refs[0].shape[0]
    for way in range(ways):
        out_ref[way * rows:(way + 1) * rows] = refs[way][...]


def join(arrays, tile, *earlier):
    ways = len(arrays)
    rows, width = arrays[0].shape
    return pl.pallas_call(
        functools.partial(join_kernel, ways),
        grid=(width // tile,),
        in_specs=[pl.BlockSpec((rows, tile), lambda n: (0, n))] * ways
        + [pl.BlockSpec(memory_space=pl.ANY)] * len(earlier),
        out_specs=pl.BlockSpec((ways * rows, tile), lambda n: (0, n)),
        out_shape=jax.ShapeDtypeStruct((ways * rows, width), arrays[0].dtype),
        compiler_params=pltpu.CompilerParams(vmem_limit_bytes=32 * MIB),
        cost_estimate=pl.CostEstimate(flops=0, bytes_accessed=0, transcendentals=0),
    )(*arrays, *earlier)


def per_device(ways, resid, spatial_q, spatial_k, spatial_v, out_weight, norm_gain, qkv_weight):
    frames, clips, rows, model = resid.shape
    patches, width = spatial_q.shape[2:]
    share = rows // ways
    tile = 1024

    plane, home, place = lax.axis_index("clip"), lax.axis_index("tm"), lax.axis_index("tensor")
    where = jnp.stack([place // 2, place % 2, home, plane]).astype(jnp.int32)

    def other_core(array):
        return lax.ppermute(array, "tensor", [(0, 1), (1, 0), (2, 3), (3, 2)])

    def other_side(array):
        return lax.ppermute(array, "tensor", [(0, 2), (2, 0), (1, 3), (3, 1)])

    def other_plane(array):
        return lax.ppermute(array, "clip", [(0, 1), (1, 0)])

    def along(array, way):
        return lax.ppermute(array, "tm", [(n, (n + way) % ways) for n in range(ways)])

    def norm_of(clip, written, *earlier):
        return norm(
            where, *attended[clip], out_weight, other_weight, branches[clip], resid, gain,
            written, clip, tile, ways, earlier,
        )

    weight = qkv_weight.transpose(1, 0, 2)
    gain = norm_gain.reshape(1, model)
    near, far = [], []

    other_weight = other_core(out_weight)
    start = columns_of(where, weight)
    near.append(along(start, 1))
    keep, send = spatial(where, spatial_q, spatial_k, spatial_v, 0, rows, [start])
    attended = [(keep, other_core(send))]
    first = branch_for_other(where, *attended[0], out_weight, other_weight, tile, [])
    branches = [other_side(first)]
    keep, send = spatial(where, spatial_q, spatial_k, spatial_v, 1, rows, [first])
    attended.append((keep, other_core(send)))
    second = branch_for_other(where, *attended[1], out_weight, other_weight, tile, [])
    (near[0],) = after([near[0]], second)
    far.append(other_plane(near[0]))
    near.append(along(near[0], 1))
    (second,) = after([second], branches[0], near[0])
    branches.append(other_side(second))
    resid_out, *normed = norm_of(0, [], second)
    moved = [[normed[0]] + [along(normed[way], way) for way in range(1, ways)]]
    (near[1],) = after([near[1]], normed[0])
    far.append(other_plane(near[1]))
    resid_out, *normed = norm_of(1, [resid_out], near[1], far[0])
    moved.append([normed[0]] + [along(normed[way], way) for way in range(1, ways)])
    mine, beside, across = [], [], [None, None]

    def gather(clip, *earlier):
        mine.append(join(moved[clip], tile, *earlier))
        beside.append(other_side(mine[clip]))

    def project_of(clip, other, *earlier):
        pieces = [mine[clip], beside[clip], *across[clip]]
        arrays = far if other else near
        block = weight.shape[1]
        came = [(1, 0, arrays[0]), (2, 0, arrays[1]), (3, 0, arrays[2]), (3, block // 2, arrays[3])]
        return project(where, pieces, weight, came, other, ways, share, earlier)

    arrived = [[], []]

    def give_back(clip, contexts, *earlier):
        leaving = after(contexts[1:], *earlier) if earlier else contexts[1:]
        arrived[clip].append([contexts[0]] + [
            along(leaving[way - 1], ways - way) for way in range(1, ways)
        ])
        return contexts[0]

    gather(0, normed[0])
    gather(1, beside[0])
    half = weight.shape[1] // 2
    mine[0], beside[0], near[1] = after([mine[0], beside[0], near[1]], mine[1], far[1])
    near.append(along(near[1][:half], 1))
    near.append(along(near[1][half:], 1))
    across[0] = [other_core(mine[0]), other_core(beside[0])]
    (near[2],) = after([near[2]], *across[0])
    far.append(other_plane(near[2]))
    mine[1], beside[1], near[3] = after([mine[1], beside[1], near[3]], near[2])
    across[1] = [other_core(mine[1]), other_core(beside[1])]
    far.append(other_plane(near[3]))
    latest = give_back(0, project_of(0, False, near[3]))
    latest = give_back(1, project_of(1, False, latest), *arrived[0][0])
    latest = give_back(0, project_of(0, True, latest), *arrived[1][0])
    latest = give_back(1, project_of(1, True, latest), *arrived[0][1])
    ordered = [
        [[got[0]] + [got[ways - way] for way in range(1, ways)] for got in by_group]
        for by_group in arrived
    ]
    temporal_ctx = assemble(where, ordered, frames, patches, share)
    return (resid_out, temporal_ctx)


def solution(mesh):
    placed = (
        P("tm", "clip", "tensor", None),
        P("tm", "clip", None, "tensor"),
        P("tm", "clip", None, "tensor"),
        P("tm", "clip", None, "tensor"),
        P("tensor", None),
        P(),
        P("tm", None, "tensor"),
    )
    small = mesh.shape["clip"] == 2 and mesh.shape["tm"] == 4 and mesh.shape["tensor"] == 4
    return jax.shard_map(
        functools.partial(per_device, mesh.shape["tm"]) if small else per_device_plain,
        mesh=mesh,
        in_specs=placed,
        out_specs=(P("tm", "clip", "tensor", None), P("tm", "clip", None, "tensor")),
        check_vma=False,
    )
```
